32 devices in a mesh: dec: 8 (over z, core), tp: 4 (over y, x).
Axes of the slice: x: 2, y: 2, z: 4, core: 2. Of those that a mesh axis runs over, the one named last changes fastest.
Arguments:
- hidden: float32 [8, 8, 4, 4096], P('dec', 'tp'), may hold values from -500 to 500
- norm_gain: float32 [4096], replicated, may hold values from 0.5 to 1.5
- lm_head: bfloat16 [16384, 4096], P(('dec', 'tp')), may hold values from -1 to 1
- token_ids: int32 [8, 8, 4], P('dec'), may hold values from 0 to 16383
- doc_counts: int32 [8], P('dec'), may hold values from 2 to 8, as said below
Outputs:
- hyp_score: float32 [8, 8], P('dec', 'tp')
- posterior: float32 [8, 8], P('dec', 'tp')
The draws below stay inside these ranges and needn't reach their ends.
Inputs may be any that keep to these rules, and one draw needn't show every extreme that they name: Document d's live hypotheses are its slots 0 to doc_counts[d] - 1; some document has 8.
All inputs are finite; a program needn't handle non-finite values.
Results may differ from the reference program's by a relative error of at most 0.0021.
Values may be sent and summed in bfloat16 or wider, within the bound.
A program may use at most 64 MiB of HBM per device.

```python
import math
import jax
import jax.numpy as jnp
from jax import lax

D = 4096
LEN = 4
VOCAB = 16384
HYP_SLOT = 8
HYP_CAP = 8
DOCS = 8


def log_uniform(key, shape, low, high):
    return jnp.exp(jax.random.uniform(key, shape, jnp.float32, math.log(low), math.log(high)))


def draw_lm_head(key, part):
    row_scale = log_uniform(jax.random.fold_in(key, 1), (VOCAB, 1), 1.0, 10.0)
    entries = jnp.clip(jax.random.normal(jax.random.fold_in(key, 2), (VOCAB, D), jnp.float32), -5.0, 5.0)
    weights = entries * row_scale / D ** 0.5
    return weights.astype(jnp.bfloat16)


def draw_hidden(key, part):
    shape = (DOCS, HYP_SLOT, LEN, D)
    col_scale = log_uniform(jax.random.fold_in(key, 11), (D,), 1.0, 10.0)
    row_scale = log_uniform(jax.random.fold_in(key, 12), (DOCS, HYP_SLOT, LEN, 1), 1.0, 10.0)
    entries = jnp.clip(jax.random.normal(jax.random.fold_in(key, 14), shape, jnp.float32), -5.0, 5.0)
    values = entries * row_scale * col_scale
    return values


def draw_doc_counts(key, part):
    values = jax.random.randint(jax.random.fold_in(key, 21), (DOCS,), HYP_SLOT // 4, HYP_CAP + 1, jnp.int32)
    fullest = jax.random.randint(jax.random.fold_in(key, 22), (), 0, DOCS, jnp.int32)
    return values.at[fullest].set(HYP_CAP)


def set_ends(values, rng, low, top_value):
    place = [jax.random.randint(jax.random.fold_in(rng, axis), (), 0, length) for axis, length in enumerate(values.shape)]
    longest = values.shape.index(max(values.shape))
    beside = place[:longest] + [(place[longest] + 1) % values.shape[longest]] + place[longest + 1:]
    return values.at[tuple(place)].set(low).at[tuple(beside)].set(top_value)


def setup_inputs(seed: int = 0) -> dict:
    key_of = jax.random.split(jax.random.key(seed), 6)
    return {
        "hidden": draw_hidden(jax.random.fold_in(key_of[5], 71), 0),
        "norm_gain": jnp.clip(1.0 + 0.1 * jax.random.normal(key_of[1], (D,), jnp.float32), 0.5, 1.5),
        "lm_head": draw_lm_head(jax.random.fold_in(key_of[5], 71), 0),
        "token_ids": set_ends(jax.random.randint(key_of[3], (DOCS, HYP_SLOT, LEN), 0, VOCAB), jax.random.fold_in(key_of[3], 1), 0, VOCAB - 1).astype(jnp.int32),
        "doc_counts": draw_doc_counts(jax.random.fold_in(key_of[5], 71), 0),
    }


def reference(hidden, norm_gain, lm_head, token_ids, doc_counts):
    flat = hidden.reshape(-1, D)
    meansq = lax.optimization_barrier(jnp.mean(flat * flat, axis=1, keepdims=True))
    normed = (flat * lax.rsqrt(meansq + 1e-05) * norm_gain).astype(jnp.bfloat16)
    flat_ids = token_ids.reshape(-1).astype(jnp.int32)
    total_rows = flat.shape[0]
    block_size = math.gcd(total_rows, 256)

    def score_block(inputs):
        block_rows, block_ids = inputs
        logits = lax.dot_general(block_rows, lm_head, (((1,), (1,)), ((), ())), preferred_element_type=jnp.float32)
        log_total = jax.nn.logsumexp(logits, axis=1)
        target = jnp.take_along_axis(logits, block_ids[:, None], axis=1)[:, 0]
        return target - log_total
    token_logp = lax.map(score_block, (normed.reshape(-1, block_size, D), flat_ids.reshape(-1, block_size)))
    token_logp = token_logp.reshape(DOCS, HYP_SLOT, LEN)
    score = lax.optimization_barrier(jnp.sum(token_logp, axis=2)) / LEN
    slot_ids = jnp.arange(HYP_SLOT, dtype=jnp.int32)
    alive = slot_ids[None, :] < doc_counts[:, None]
    best_score = lax.optimization_barrier(jnp.max(jnp.where(alive, score, -jnp.inf), axis=1, keepdims=True))
    doc_norm = best_score + jnp.log(lax.optimization_barrier(jnp.sum(jnp.exp(jnp.where(alive, score - best_score, -jnp.inf)), axis=1, keepdims=True)))
    hyp_score = jnp.where(alive, score, 0.0)
    posterior = jnp.where(alive, score - doc_norm, 0.0)
    return (hyp_score, posterior)
```

```python
import functools

import jax
import jax.numpy as jnp
from jax import lax
from jax.experimental import pallas as pl
from jax.experimental.pallas import tpu as pltpu
from jax.sharding import PartitionSpec as P

MESH = pl.DeviceIdType.MESH
CORES = 2
HALVES = 2
EPS = 1e-05


def flip(index, mask):
    bit = 1
    while bit <= mask:
        if mask & bit:
            index = index + bit - 2 * bit * ((index // bit) % 2)
        bit *= 2
    return index


def kernel(dec_n, tp_n, hidden, gain, lm_head, ids, counts, hyp_ref, post_ref,
           weights, rows, doc_ids, id_row, fresh, logits, stat_row, stats, got_dec, stat_doc, got_tp,
           w_sem, send_sem, recv_sem, id_send, id_recv, dec_send, dec_recv, tp_send, tp_recv):
    slots, length, width = hidden.shape[1:]
    own_rows = slots * length
    doc_rows = tp_n * own_rows
    vocab = lm_head.shape[0]
    devices = dec_n * tp_n
    z_n = dec_n // CORES
    x_n = 2 ** ((tp_n.bit_length()) // 2)
    y_n = tp_n // x_n
    half = width // HALVES
    dec, tp = lax.axis_index("dec"), lax.axis_index("tp")
    z, core = dec // CORES, dec % CORES
    y, x = tp // x_n, tp % x_n
    me = dec * tp_n + tp

    barrier = pltpu.get_barrier_semaphore()
    for d in range(1, dec_n):
        pl.semaphore_signal(barrier, inc=1, device_id=(flip(dec, d), tp), device_id_type=MESH)
    for d in range(1, tp_n):
        pl.semaphore_signal(barrier, inc=1, device_id=(dec, flip(tp, d)), device_id_type=MESH)
    load = pltpu.make_async_copy(lm_head, weights, w_sem)
    load.start()

    for s in range(slots):
        part = hidden[0, s]
        meansq = jnp.mean(part * part, axis=1, keepdims=True)
        fresh[s * length:(s + 1) * length, :] = part * lax.rsqrt(meansq + EPS) * gain[...]
    rows[me] = fresh[...].astype(jnp.bfloat16)

    lane = lax.broadcasted_iota(jnp.int32, (doc_ids.shape[1], 128), 1)
    slot = lax.broadcasted_iota(jnp.int32, (doc_ids.shape[1], 128), 0)
    values = ids[0].astype(jnp.float32)
    spread = jnp.zeros((doc_ids.shape[1], 128), jnp.float32)
    for l in range(length):
        spread = jnp.where(lane == slot * length + l, values[:, l:l + 1], spread)
    doc_ids[dec] = jnp.broadcast_to(jnp.sum(spread, axis=0, keepdims=True), spread.shape)
    stats[...] = jnp.zeros_like(stats)
    stat_doc[...] = jnp.zeros_like(stat_doc)

    pl.semaphore_wait(barrier, dec_n + tp_n - 2)

    def block(zz, cc, yy, xx):
        return (zz * CORES + cc) * tp_n + yy * x_n + xx

    def send(b, h, to_dec, to_tp):
        part = rows.at[b, :, pl.ds(h * half, half)]
        pltpu.make_async_remote_copy(
            src_ref=part, dst_ref=part, send_sem=send_sem, recv_sem=recv_sem.at[b, h],
            device_id=(to_dec, to_tp), device_id_type=MESH).start()

    def take(b, h):
        part = rows.at[b, :, pl.ds(h * half, half)]
        pltpu.make_async_copy(part, part, recv_sem.at[b, h]).wait()

    x_peers = [y * x_n + flip(x, d) for d in range(1, x_n)]
    y_peers = [flip(y, d) * x_n + x for d in range(1, y_n)]
    mate = flip(dec, 1)

    def send_x(b, h):
        for peer in x_peers:
            send(b, h, dec, peer)

    def send_y(b, h):
        for peer in y_peers:
            send(b, h, dec, peer)

    for h in range(HALVES):
        for d in range(1, z_n):
            send(me, h, flip(z, d) * CORES + core, tp)
        send_x(me, h)
        send_y(me, h)
        send(me, h, mate, tp)
        if h == 0:
            for d in range(1, dec_n):
                pltpu.make_async_remote_copy(
                    src_ref=doc_ids.at[dec], dst_ref=doc_ids.at[dec], send_sem=id_send,
                    recv_sem=id_recv, device_id=(flip(dec, d), tp), device_id_type=MESH).start()

    for h in range(HALVES):
        for d in range(z_n):
            zz = flip(z, d)
            if d:
                b = block(zz, core, y, x)
                take(b, h)
                send_x(b, h)
                send_y(b, h)
                send(b, h, mate, tp)
            for e in range(1, x_n):
                b = block(zz, core, y, flip(x, e))
                take(b, h)
                if h == 0:
                    send_y(b, h)
                send(b, h, mate, tp)
            for e in range(1, y_n):
                b = block(zz, core, flip(y, e), x)
                take(b, h)
                if h == 1:
                    send_x(b, h)
                send(b, h, mate, tp)
        for d in range(z_n):
            for e in range(1, x_n):
                for f in range(1, y_n):
                    b = block(flip(z, d), core, flip(y, f), flip(x, e))
                    take(b, h)
                    send(b, h, mate, tp)
    others = pltpu.make_async_copy(doc_ids.at[0:dec_n - 1], doc_ids.at[0:dec_n - 1], id_recv)
    others.wait()
    load.wait()
    for h in range(HALVES):
        for d in range(z_n):
            for e in range(x_n):
                for f in range(y_n):
                    take(block(flip(z, d), 1 - core, flip(y, f), flip(x, e)), h)

    for g in range(dec_n):
        id_row[0:1, g * doc_rows:(g + 1) * doc_rows] = doc_ids[g, 0:1, 0:doc_rows]

    total = devices * own_rows
    tile = min(256, total)
    blocks = tile // own_rows
    step = 512
    vocab_start = (dec * tp_n + tp) * vocab

    @pl.loop(0, total // tile)
    def _(t):
        logits[...] = jnp.zeros((vocab, tile), jnp.float32)

        @pl.loop(0, width // step)
        def _(k):
            at = pl.ds(pl.multiple_of(k * step, step), step)
            part = rows[pl.ds(t * blocks, blocks), :, at].astype(jnp.float32)
            part = part.reshape(tile, step).astype(jnp.bfloat16)
            logits[...] += lax.dot_general(
                weights[:, at], part, (((1,), (1,)), ((), ())),
                preferred_element_type=jnp.float32)

        value = logits[...]
        peak = jnp.max(value, axis=0, keepdims=True)
        place = pl.ds(pl.multiple_of(t * tile, tile), tile)
        entry = (lax.broadcasted_iota(jnp.int32, (vocab, tile), 0) + vocab_start).astype(jnp.float32)
        stat_row[0:1, place] = peak
        stat_row[1:2, place] = jnp.sum(jnp.exp(value - peak), axis=0, keepdims=True)
        stat_row[2:3, place] = jnp.sum(
            jnp.where(entry == id_row[0:1, place], value, 0.0), axis=0, keepdims=True)

    for g in range(dec_n):
        stats[g, 0:3, 0:doc_rows] = stat_row[0:3, g * doc_rows:(g + 1) * doc_rows]
    got_dec[dec] = stats[dec]
    for d in range(1, dec_n):
        to = flip(dec, d)
        pltpu.make_async_remote_copy(
            src_ref=stats.at[to], dst_ref=got_dec.at[dec], send_sem=dec_send,
            recv_sem=dec_recv, device_id=(to, tp), device_id_type=MESH).start()
    come = pltpu.make_async_copy(got_dec.at[0:dec_n - 1], got_dec.at[0:dec_n - 1], dec_recv)
    come.wait()

    def merged(got):
        peak = jnp.max(got[:, 0:1, :], axis=0)
        summed = jnp.sum(got[:, 1:2, :] * jnp.exp(got[:, 0:1, :] - peak[None]), axis=0)
        return peak, summed, jnp.sum(got[:, 2:3, :], axis=0)

    for i, value in enumerate(merged(got_dec[...])):
        stat_doc[i:i + 1, :] = value
    got_tp[tp] = stat_doc[...]
    for d in range(1, tp_n):
        pltpu.make_async_remote_copy(
            src_ref=stat_doc, dst_ref=got_tp.at[tp], send_sem=tp_send,
            recv_sem=tp_recv, device_id=(dec, flip(tp, d)), device_id_type=MESH).start()
    pltpu.make_async_copy(got_tp.at[0:tp_n - 1], got_tp.at[0:tp_n - 1], tp_recv).wait()
    peak, summed, target = merged(got_tp[...])

    logp = target - (peak + jnp.log(summed))
    score = logp
    for l in range(1, length):
        score = score + pltpu.roll(logp, 128 - l, 1)
    score = score / length
    lane = lax.broadcasted_iota(jnp.int32, (1, 128), 1)
    first = jnp.logical_and(lane % length == 0, lane < doc_rows)
    alive = jnp.logical_and(first, lane // length < counts[0])
    best = jnp.max(jnp.where(alive, score, -jnp.inf), axis=1, keepdims=True)
    norm = best + jnp.log(jnp.sum(
        jnp.exp(jnp.where(alive, score - best, -jnp.inf)), axis=1, keepdims=True))
    hyp = jnp.where(alive, score, 0.0)
    post = jnp.where(alive, score - norm, 0.0)
    out_lane = lax.broadcasted_iota(jnp.int32, (1, slots), 1)
    hyp_out = jnp.zeros((1, slots), jnp.float32)
    post_out = jnp.zeros((1, slots), jnp.float32)
    for s in range(slots):
        here = lane == (tp * slots + s) * length
        hyp_out = jnp.where(out_lane == s, jnp.sum(jnp.where(here, hyp, 0.0), axis=1, keepdims=True), hyp_out)
        post_out = jnp.where(out_lane == s, jnp.sum(jnp.where(here, post, 0.0), axis=1, keepdims=True), post_out)
    hyp_ref[...] = hyp_out
    post_ref[...] = post_out

    sent = rows.at[0:devices - 1]
    pltpu.make_async_copy(sent, sent, send_sem).wait()
    pltpu.make_async_copy(doc_ids.at[0:dec_n - 1], doc_ids.at[0:dec_n - 1], id_send).wait()
    pltpu.make_async_copy(got_dec.at[0:dec_n - 1], got_dec.at[0:dec_n - 1], dec_send).wait()
    pltpu.make_async_copy(got_tp.at[0:tp_n - 1], got_tp.at[0:tp_n - 1], tp_send).wait()


def body(dec_n, tp_n, hidden, norm_gain, lm_head, token_ids, doc_counts):
    slots, length, width = hidden.shape[1:]
    own_rows = slots * length
    devices = dec_n * tp_n
    vocab = lm_head.shape[0]
    total = devices * own_rows
    all_slots = token_ids.shape[1]
    vmem = pl.BlockSpec(memory_space=pltpu.VMEM)
    out = jax.ShapeDtypeStruct((1, slots), jnp.float32)
    dma = pltpu.SemaphoreType.DMA
    return pl.pallas_call(
        functools.partial(kernel, dec_n, tp_n),
        out_shape=(out, out),
        in_specs=[vmem, vmem, pl.BlockSpec(memory_space=pl.ANY), vmem,
                  pl.BlockSpec(memory_space=pltpu.SMEM)],
        out_specs=(vmem, vmem),
        scratch_shapes=[
            pltpu.VMEM((vocab, width), jnp.bfloat16),
            pltpu.VMEM((devices, own_rows, width), jnp.bfloat16),
            pltpu.VMEM((dec_n, all_slots, 128), jnp.float32),
            pltpu.VMEM((8, total), jnp.float32),
            pltpu.VMEM((own_rows, width), jnp.float32),
            pltpu.VMEM((vocab, min(256, total)), jnp.float32),
            pltpu.VMEM((8, total), jnp.float32),
            pltpu.VMEM((dec_n, 8, 128), jnp.float32),
            pltpu.VMEM((dec_n, 8, 128), jnp.float32),
            pltpu.VMEM((8, 128), jnp.float32),
            pltpu.VMEM((tp_n, 8, 128), jnp.float32),
            dma, dma, dma((devices, HALVES)), dma, dma, dma, dma, dma, dma,
        ],
        compiler_params=pltpu.CompilerParams(
            collective_id=0, has_side_effects=True, vmem_limit_bytes=48 * 1024 * 1024),
        name="rescore",
    )(hidden, norm_gain.reshape(1, width), lm_head, token_ids, doc_counts)


def solution(mesh):
    placed = (
        P("dec", "tp", None, None),
        P(),
        P(("dec", "tp"), None),
        P("dec", None, None),
        P("dec"),
    )
    return jax.shard_map(
        functools.partial(body, mesh.shape["dec"], mesh.shape["tp"]),
        mesh=mesh,
        in_specs=placed,
        out_specs=(P("dec", "tp"), P("dec", "tp")),
        check_vma=False,
    )
```

```python
import functools

import jax
import jax.numpy as jnp
from jax import lax
from jax.experimental import pallas as pl
from jax.experimental.pallas import tpu as pltpu
from jax.sharding import PartitionSpec as P

MESH = pl.DeviceIdType.MESH
CORES = 2
HALVES = 2
EPS = 1e-05


def flip(index, mask):
    bit = 1
    while bit <= mask:
        if mask & bit:
            index = index + bit - 2 * bit * ((index // bit) % 2)
        bit *= 2
    return index


def kernel(dec_n, tp_n, hidden_hbm, gain_hbm, lm_head, ids_hbm, counts, hyp_ref, post_ref,
           hidden, gain, ids, weights, rows, doc_ids, id_row, fresh, logits, stat_row, stats, got_dec, stat_doc, got_tp,
           h_sem, g_sem, i_sem, w_sem, send_sem, recv_sem, id_send, id_recv, dec_send, dec_recv, tp_send, tp_recv):
    slots, length, width = hidden.shape[1:]
    own_rows = slots * length
    doc_rows = tp_n * own_rows
    vocab = lm_head.shape[0]
    devices = dec_n * tp_n
    z_n = dec_n // CORES
    x_n = 2 ** ((tp_n.bit_length()) // 2)
    assert x_n * x_n == tp_n
    half = width // HALVES
    dec, tp = lax.axis_index("dec"), lax.axis_index("tp")
    z, core = dec // CORES, dec % CORES
    u_step = 1 + core * (x_n - 1)
    v_step = x_n - core * (x_n - 1)
    u, v = (tp // u_step) % x_n, (tp // v_step) % x_n
    me = dec * tp_n + tp

    barrier = pltpu.get_barrier_semaphore()
    for d in range(1, dec_n):
        pl.semaphore_signal(barrier, inc=1, device_id=(flip(dec, d), tp), device_id_type=MESH)
    for d in range(1, tp_n):
        pl.semaphore_signal(barrier, inc=1, device_id=(dec, flip(tp, d)), device_id_type=MESH)
    loads = [pltpu.make_async_copy(*pair) for pair in (
        (hidden_hbm, hidden, h_sem), (gain_hbm, gain, g_sem), (ids_hbm, ids, i_sem), (lm_head, weights, w_sem))]
    for load in loads:
        load.start()
    for load in loads[:3]:
        load.wait()

    for s in range(slots):
        part = hidden[0, s]
        meansq = jnp.mean(part * part, axis=1, keepdims=True)
        fresh[s * length:(s + 1) * length, :] = part * lax.rsqrt(meansq + EPS) * gain[...]
    rows[me] = fresh[...].astype(jnp.bfloat16)

    all_slots = ids.shape[2]
    lane = lax.broadcasted_iota(jnp.int32, (length, 128), 1)
    token = lax.broadcasted_iota(jnp.int32, (length, 128), 0)
    values = ids[0].astype(jnp.float32)
    spread = jnp.zeros((length, 128), jnp.float32)
    for s in range(all_slots):
        spread = jnp.where(lane == s * length + token, values[:, s:s + 1], spread)
    doc_ids[dec] = jnp.broadcast_to(jnp.sum(spread, axis=0, keepdims=True), doc_ids.shape[1:])
    stats[...] = jnp.zeros_like(stats)
    stat_doc[...] = jnp.zeros_like(stat_doc)

    pl.semaphore_wait(barrier, dec_n + tp_n - 2)

    def block(zz, cc, vv, uu):
        return (zz * CORES + cc) * tp_n + vv * v_step + uu * u_step

    def send(b, h, to_dec, to_tp):
        part = rows.at[b, :, pl.ds(h * half, half)]
        pltpu.make_async_remote_copy(
            src_ref=part, dst_ref=part, send_sem=send_sem, recv_sem=recv_sem.at[b, h],
            device_id=(to_dec, to_tp), device_id_type=MESH).start()

    def send_mate(b):
        pltpu.make_async_remote_copy(
            src_ref=rows.at[b], dst_ref=rows.at[b], send_sem=send_sem, recv_sem=recv_sem.at[b, 0],
            device_id=(flip(dec, 1), tp), device_id_type=MESH).start()

    def take(b, h):
        part = rows.at[b, :, pl.ds(h * half, half)]
        pltpu.make_async_copy(part, part, recv_sem.at[b, h]).wait()

    def send_u(b, h):
        for d in range(1, x_n):
            send(b, h, dec, v * v_step + flip(u, d) * u_step)

    def send_v(b, h):
        for d in range(1, x_n):
            send(b, h, dec, flip(v, d) * v_step + u * u_step)

    for h in range(HALVES):
        send_u(me, h)
        for d in range(1, z_n):
            send(me, h, flip(z, d) * CORES + core, tp)
        send_v(me, h)
    send_mate(me)
    for d in range(1, dec_n):
        pltpu.make_async_remote_copy(
            src_ref=doc_ids.at[dec], dst_ref=doc_ids.at[dec], send_sem=id_send,
            recv_sem=id_recv, device_id=(flip(dec, d), tp), device_id_type=MESH).start()

    for h in range(HALVES):
        for d in range(z_n):
            zz = flip(z, d)
            if d:
                b = block(zz, core, v, u)
                take(b, h)
                send_u(b, h)
                send_v(b, h)
                if h == 1:
                    send_mate(b)
            for e in range(1, x_n):
                b = block(zz, core, v, flip(u, e))
                take(b, h)
                if h == 0:
                    send_v(b, h)
                else:
                    send_mate(b)
            for e in range(1, x_n):
                b = block(zz, core, flip(v, e), u)
                take(b, h)
                if h == 1:
                    send_u(b, h)
                    send_mate(b)
    for d in range(z_n):
        for e in range(1, x_n):
            for f in range(1, x_n):
                b = block(flip(z, d), core, flip(v, f), flip(u, e))
                for h in range(HALVES):
                    take(b, h)
                send_mate(b)
    others = pltpu.make_async_copy(doc_ids.at[0:dec_n - 1], doc_ids.at[0:dec_n - 1], id_recv)
    others.wait()
    loads[3].wait()
    for d in range(z_n):
        for e in range(x_n):
            for f in range(x_n):
                b = block(flip(z, d), 1 - core, flip(v, f), flip(u, e))
                pltpu.make_async_copy(rows.at[b], rows.at[b], recv_sem.at[b, 0]).wait()

    for g in range(dec_n):
        id_row[0:1, g * doc_rows:(g + 1) * doc_rows] = doc_ids[g, 0:1, 0:doc_rows]

    total = devices * own_rows
    tile = min(256, total)
    blocks = tile // own_rows
    step = 512
    vocab_start = (dec * tp_n + tp) * vocab

    @pl.loop(0, total // tile)
    def _(t):
        logits[...] = jnp.zeros((vocab, tile), jnp.float32)

        @pl.loop(0, width // step)
        def _(k):
            at = pl.ds(pl.multiple_of(k * step, step), step)
            part = rows[pl.ds(t * blocks, blocks), :, at].astype(jnp.float32)
            part = part.reshape(tile, step).astype(jnp.bfloat16)
            logits[...] += lax.dot_general(
                weights[:, at], part, (((1,), (1,)), ((), ())),
                preferred_element_type=jnp.float32)

        value = logits[...]
        peak = jnp.max(value, axis=0, keepdims=True)
        place = pl.ds(pl.multiple_of(t * tile, tile), tile)
        entry = (lax.broadcasted_iota(jnp.int32, (vocab, tile), 0) + vocab_start).astype(jnp.float32)
        stat_row[0:1, place] = peak
        stat_row[1:2, place] = jnp.sum(jnp.exp(value - peak), axis=0, keepdims=True)
        stat_row[2:3, place] = jnp.sum(
            jnp.where(entry == id_row[0:1, place], value, 0.0), axis=0, keepdims=True)

    for g in range(dec_n):
        stats[g, 0:3, 0:doc_rows] = stat_row[0:3, g * doc_rows:(g + 1) * doc_rows]
    got_dec[dec] = stats[dec]
    for d in range(1, dec_n):
        to = flip(dec, d)
        pltpu.make_async_remote_copy(
            src_ref=stats.at[to], dst_ref=got_dec.at[dec], send_sem=dec_send,
            recv_sem=dec_recv, device_id=(to, tp), device_id_type=MESH).start()
    come = pltpu.make_async_copy(got_dec.at[0:dec_n - 1], got_dec.at[0:dec_n - 1], dec_recv)
    come.wait()

    def merged(got):
        peak = jnp.max(got[:, 0:1, :], axis=0)
        summed = jnp.sum(got[:, 1:2, :] * jnp.exp(got[:, 0:1, :] - peak[None]), axis=0)
        return peak, summed, jnp.sum(got[:, 2:3, :], axis=0)

    for i, value in enumerate(merged(got_dec[...])):
        stat_doc[i:i + 1, :] = value
    got_tp[tp] = stat_doc[...]
    for d in range(1, tp_n):
        pltpu.make_async_remote_copy(
            src_ref=stat_doc, dst_ref=got_tp.at[tp], send_sem=tp_send,
            recv_sem=tp_recv, device_id=(dec, flip(tp, d)), device_id_type=MESH).start()
    pltpu.make_async_copy(got_tp.at[0:tp_n - 1], got_tp.at[0:tp_n - 1], tp_recv).wait()
    peak, summed, target = merged(got_tp[...])

    logp = target - (peak + jnp.log(summed))
    score = logp
    for l in range(1, length):
        score = score + pltpu.roll(logp, 128 - l, 1)
    score = score / length
    lane = lax.broadcasted_iota(jnp.int32, (1, 128), 1)
    first = jnp.logical_and(lane % length == 0, lane < doc_rows)
    alive = jnp.logical_and(first, lane // length < counts[0])
    best = jnp.max(jnp.where(alive, score, -jnp.inf), axis=1, keepdims=True)
    norm = best + jnp.log(jnp.sum(
        jnp.exp(jnp.where(alive, score - best, -jnp.inf)), axis=1, keepdims=True))
    hyp = jnp.where(alive, score, 0.0)
    post = jnp.where(alive, score - norm, 0.0)
    out_lane = lax.broadcasted_iota(jnp.int32, (1, slots), 1)
    hyp_out = jnp.zeros((1, slots), jnp.float32)
    post_out = jnp.zeros((1, slots), jnp.float32)
    for s in range(slots):
        here = lane == (tp * slots + s) * length
        hyp_out = jnp.where(out_lane == s, jnp.sum(jnp.where(here, hyp, 0.0), axis=1, keepdims=True), hyp_out)
        post_out = jnp.where(out_lane == s, jnp.sum(jnp.where(here, post, 0.0), axis=1, keepdims=True), post_out)
    hyp_ref[...] = hyp_out
    post_ref[...] = post_out

    sent = rows.at[0:devices - 1]
    pltpu.make_async_copy(sent, sent, send_sem).wait()
    pltpu.make_async_copy(doc_ids.at[0:dec_n - 1], doc_ids.at[0:dec_n - 1], id_send).wait()
    pltpu.make_async_copy(got_dec.at[0:dec_n - 1], got_dec.at[0:dec_n - 1], dec_send).wait()
    pltpu.make_async_copy(got_tp.at[0:tp_n - 1], got_tp.at[0:tp_n - 1], tp_send).wait()


def body(dec_n, tp_n, hidden, norm_gain, lm_head, token_ids, doc_counts):
    slots, length, width = hidden.shape[1:]
    own_rows = slots * length
    devices = dec_n * tp_n
    vocab = lm_head.shape[0]
    total = devices * own_rows
    all_slots = token_ids.shape[1]
    vmem = pl.BlockSpec(memory_space=pltpu.VMEM)
    out = jax.ShapeDtypeStruct((1, slots), jnp.float32)
    dma = pltpu.SemaphoreType.DMA
    return pl.pallas_call(
        functools.partial(kernel, dec_n, tp_n),
        out_shape=(out, out),
        in_specs=[pl.BlockSpec(memory_space=pl.ANY)] * 4 + [pl.BlockSpec(memory_space=pltpu.SMEM)],
        out_specs=(vmem, vmem),
        scratch_shapes=[
            pltpu.VMEM(hidden.shape, jnp.float32),
            pltpu.VMEM((1, width), jnp.float32),
            pltpu.VMEM((1, length, all_slots), jnp.int32),
            pltpu.VMEM((vocab, width), jnp.bfloat16),
            pltpu.VMEM((devices, own_rows, width), jnp.bfloat16),
            pltpu.VMEM((dec_n, 8, 128), jnp.float32),
            pltpu.VMEM((8, total), jnp.float32),
            pltpu.VMEM((own_rows, width), jnp.float32),
            pltpu.VMEM((vocab, min(256, total)), jnp.float32),
            pltpu.VMEM((8, total), jnp.float32),
            pltpu.VMEM((dec_n, 8, 128), jnp.float32),
            pltpu.VMEM((dec_n, 8, 128), jnp.float32),
            pltpu.VMEM((8, 128), jnp.float32),
            pltpu.VMEM((tp_n, 8, 128), jnp.float32),
            dma, dma, dma, dma, dma, dma((devices, HALVES)), dma, dma, dma, dma, dma, dma,
        ],
        compiler_params=pltpu.CompilerParams(
            collective_id=0, has_side_effects=True, vmem_limit_bytes=60 * 1024 * 1024),
        name="rescore",
    )(hidden, norm_gain.reshape(1, width), lm_head, jnp.swapaxes(token_ids, 1, 2), doc_counts)


def solution(mesh):
    placed = (
        P("dec", "tp", None, None),
        P(),
        P(("dec", "tp"), None),
        P("dec", None, None),
        P("dec"),
    )
    return jax.shard_map(
        functools.partial(body, mesh.shape["dec"], mesh.shape["tp"]),
        mesh=mesh,
        in_specs=placed,
        out_specs=(P("dec", "tp"), P("dec", "tp")),
        check_vma=False,
    )
```

```python
import functools

import jax
import jax.numpy as jnp
from jax import lax
from jax.experimental import pallas as pl
from jax.experimental.pallas import tpu as pltpu
from jax.sharding import PartitionSpec as P

MESH = pl.DeviceIdType.MESH
CORES = 2
HALVES = 2
EPS = 1e-05


def flip(index, mask):
    bit = 1
    while bit <= mask:
        if mask & bit:
            index = index + bit - 2 * bit * ((index // bit) % 2)
        bit *= 2
    return index


def gather_kernel(dec_n, tp_n, hidden_hbm, gain_hbm, ids_hbm, rows, doc_ids,
                  hidden, gain, ids, fresh, h_sem, g_sem, i_sem, send_sem, recv_sem, id_send, id_recv):
    slots, length, width = hidden.shape[1:]
    own_rows = slots * length
    doc_rows = tp_n * own_rows
    devices = dec_n * tp_n
    z_n = dec_n // CORES
    x_n = 2 ** ((tp_n.bit_length()) // 2)
    assert x_n * x_n == tp_n
    half = width // HALVES
    dec, tp = lax.axis_index("dec"), lax.axis_index("tp")
    z, core = dec // CORES, dec % CORES
    u_step = 1 + core * (x_n - 1)
    v_step = x_n - core * (x_n - 1)
    u, v = (tp // u_step) % x_n, (tp // v_step) % x_n
    me = dec * tp_n + tp

    barrier = pltpu.get_barrier_semaphore()
    for d in range(1, dec_n):
        pl.semaphore_signal(barrier, inc=1, device_id=(flip(dec, d), tp), device_id_type=MESH)
    for d in range(1, tp_n):
        pl.semaphore_signal(barrier, inc=1, device_id=(dec, flip(tp, d)), device_id_type=MESH)
    loads = [pltpu.make_async_copy(*pair) for pair in (
        (hidden_hbm, hidden, h_sem), (gain_hbm, gain, g_sem), (ids_hbm, ids, i_sem))]
    for load in loads:
        load.start()
    for load in loads:
        load.wait()

    for s in range(slots):
        part = hidden[0, s]
        meansq = jnp.mean(part * part, axis=1, keepdims=True)
        fresh[s * length:(s + 1) * length, :] = part * lax.rsqrt(meansq + EPS) * gain[...]
    rows[me] = fresh[...].astype(jnp.bfloat16)

    all_slots = ids.shape[2]
    lane = lax.broadcasted_iota(jnp.int32, (length, 128), 1)
    token = lax.broadcasted_iota(jnp.int32, (length, 128), 0)
    values = ids[0].astype(jnp.float32)
    spread = jnp.zeros((length, 128), jnp.float32)
    for s in range(all_slots):
        spread = jnp.where(lane == s * length + token, values[:, s:s + 1], spread)
    doc_ids[dec] = jnp.broadcast_to(jnp.sum(spread, axis=0, keepdims=True), doc_ids.shape[1:])

    pl.semaphore_wait(barrier, dec_n + tp_n - 2)

    def block(zz, cc, vv, uu):
        return (zz * CORES + cc) * tp_n + vv * v_step + uu * u_step

    def send(b, h, to_dec, to_tp):
        part = rows.at[b, :, pl.ds(h * half, half)]
        pltpu.make_async_remote_copy(
            src_ref=part, dst_ref=part, send_sem=send_sem, recv_sem=recv_sem.at[b, h],
            device_id=(to_dec, to_tp), device_id_type=MESH).start()

    def send_mate(b):
        pltpu.make_async_remote_copy(
            src_ref=rows.at[b], dst_ref=rows.at[b], send_sem=send_sem, recv_sem=recv_sem.at[b, 0],
            device_id=(flip(dec, 1), tp), device_id_type=MESH).start()

    def take(b, h):
        part = rows.at[b, :, pl.ds(h * half, half)]
        pltpu.make_async_copy(part, part, recv_sem.at[b, h]).wait()

    def send_u(b, h):
        for d in range(1, x_n):
            send(b, h, dec, v * v_step + flip(u, d) * u_step)

    def send_v(b, h):
        for d in range(1, x_n):
            send(b, h, dec, flip(v, d) * v_step + u * u_step)

    for h in range(HALVES):
        send_u(me, h)
        for d in range(1, z_n):
            send(me, h, flip(z, d) * CORES + core, tp)
        send_v(me, h)
    send_mate(me)
    for d in range(1, dec_n):
        pltpu.make_async_remote_copy(
            src_ref=doc_ids.at[dec], dst_ref=doc_ids.at[dec], send_sem=id_send,
            recv_sem=id_recv, device_id=(flip(dec, d), tp), device_id_type=MESH).start()

    for h in range(HALVES):
        for d in range(z_n):
            zz = flip(z, d)
            if d:
                b = block(zz, core, v, u)
                take(b, h)
                send_u(b, h)
                send_v(b, h)
                if h == 1:
                    send_mate(b)
            for e in range(1, x_n):
                b = block(zz, core, v, flip(u, e))
                take(b, h)
                if h == 0:
                    send_v(b, h)
                else:
                    send_mate(b)
            for e in range(1, x_n):
                b = block(zz, core, flip(v, e), u)
                take(b, h)
                if h == 1:
                    send_u(b, h)
                    send_mate(b)
    for d in range(z_n):
        for e in range(1, x_n):
            for f in range(1, x_n):
                b = block(flip(z, d), core, flip(v, f), flip(u, e))
                for h in range(HALVES):
                    take(b, h)
                send_mate(b)
    others = pltpu.make_async_copy(doc_ids.at[0:dec_n - 1], doc_ids.at[0:dec_n - 1], id_recv)
    others.wait()
    for d in range(z_n):
        for e in range(x_n):
            for f in range(x_n):
                b = block(flip(z, d), 1 - core, flip(v, f), flip(u, e))
                pltpu.make_async_copy(rows.at[b], rows.at[b], recv_sem.at[b, 0]).wait()

    sent = rows.at[0:devices - 1]
    pltpu.make_async_copy(sent, sent, send_sem).wait()
    pltpu.make_async_copy(doc_ids.at[0:dec_n - 1], doc_ids.at[0:dec_n - 1], id_send).wait()


def exchange_kernel(dec_n, tp_n, length, slots, stats, counts, hyp_ref, post_ref,
                    got_dec, stat_doc, got_tp, dec_send, dec_recv, tp_send, tp_recv):
    dec, tp = lax.axis_index("dec"), lax.axis_index("tp")
    doc_rows = tp_n * slots * length
    barrier = pltpu.get_barrier_semaphore()
    for d in range(1, dec_n):
        pl.semaphore_signal(barrier, inc=1, device_id=(flip(dec, d), tp), device_id_type=MESH)
    for d in range(1, tp_n):
        pl.semaphore_signal(barrier, inc=1, device_id=(dec, flip(tp, d)), device_id_type=MESH)
    stat_doc[...] = jnp.zeros_like(stat_doc)
    pl.semaphore_wait(barrier, dec_n + tp_n - 2)
    got_dec[dec] = stats[dec]
    for d in range(1, dec_n):
        to = flip(dec, d)
        pltpu.make_async_remote_copy(
            src_ref=stats.at[to], dst_ref=got_dec.at[dec], send_sem=dec_send,
            recv_sem=dec_recv, device_id=(to, tp), device_id_type=MESH).start()
    come = pltpu.make_async_copy(got_dec.at[0:dec_n - 1], got_dec.at[0:dec_n - 1], dec_recv)
    come.wait()

    def merged(got):
        peak = jnp.max(got[:, 0:1, :], axis=0)
        summed = jnp.sum(got[:, 1:2, :] * jnp.exp(got[:, 0:1, :] - peak[None]), axis=0)
        return peak, summed, jnp.sum(got[:, 2:3, :], axis=0)

    for i, value in enumerate(merged(got_dec[...])):
        stat_doc[i:i + 1, :] = value
    got_tp[tp] = stat_doc[...]
    for d in range(1, tp_n):
        pltpu.make_async_remote_copy(
            src_ref=stat_doc, dst_ref=got_tp.at[tp], send_sem=tp_send,
            recv_sem=tp_recv, device_id=(dec, flip(tp, d)), device_id_type=MESH).start()
    pltpu.make_async_copy(got_tp.at[0:tp_n - 1], got_tp.at[0:tp_n - 1], tp_recv).wait()
    peak, summed, target = merged(got_tp[...])

    logp = target - (peak + jnp.log(summed))
    score = logp
    for l in range(1, length):
        score = score + pltpu.roll(logp, 128 - l, 1)
    score = score / length
    lane = lax.broadcasted_iota(jnp.int32, (1, 128), 1)
    first = jnp.logical_and(lane % length == 0, lane < doc_rows)
    alive = jnp.logical_and(first, lane // length < counts[0])
    best = jnp.max(jnp.where(alive, score, -jnp.inf), axis=1, keepdims=True)
    norm = best + jnp.log(jnp.sum(
        jnp.exp(jnp.where(alive, score - best, -jnp.inf)), axis=1, keepdims=True))
    hyp = jnp.where(alive, score, 0.0)
    post = jnp.where(alive, score - norm, 0.0)
    out_lane = lax.broadcasted_iota(jnp.int32, (1, slots), 1)
    hyp_out = jnp.zeros((1, slots), jnp.float32)
    post_out = jnp.zeros((1, slots), jnp.float32)
    for s in range(slots):
        here = lane == (tp * slots + s) * length
        hyp_out = jnp.where(out_lane == s, jnp.sum(jnp.where(here, hyp, 0.0), axis=1, keepdims=True), hyp_out)
        post_out = jnp.where(out_lane == s, jnp.sum(jnp.where(here, post, 0.0), axis=1, keepdims=True), post_out)
    hyp_ref[...] = hyp_out
    post_ref[...] = post_out

    pltpu.make_async_copy(got_dec.at[0:dec_n - 1], got_dec.at[0:dec_n - 1], dec_send).wait()
    pltpu.make_async_copy(got_tp.at[0:tp_n - 1], got_tp.at[0:tp_n - 1], tp_send).wait()


def body(dec_n, tp_n, hidden, norm_gain, lm_head, token_ids, doc_counts):
    slots, length, width = hidden.shape[1:]
    own_rows = slots * length
    devices = dec_n * tp_n
    vocab = lm_head.shape[0]
    total = devices * own_rows
    doc_rows = total // dec_n
    all_slots = token_ids.shape[1]
    vmem = pl.BlockSpec(memory_space=pltpu.VMEM)
    out = jax.ShapeDtypeStruct((1, slots), jnp.float32)
    dma = pltpu.SemaphoreType.DMA
    rows, doc_ids = pl.pallas_call(
        functools.partial(gather_kernel, dec_n, tp_n),
        out_shape=(jax.ShapeDtypeStruct((devices, own_rows, width), jnp.bfloat16),
                   jax.ShapeDtypeStruct((dec_n, 8, 128), jnp.float32)),
        in_specs=[pl.BlockSpec(memory_space=pl.ANY)] * 3,
        out_specs=(vmem, vmem),
        scratch_shapes=[
            pltpu.VMEM(hidden.shape, jnp.float32),
            pltpu.VMEM((1, width), jnp.float32),
            pltpu.VMEM((1, length, all_slots), jnp.int32),
            pltpu.VMEM((own_rows, width), jnp.float32),
            dma, dma, dma, dma, dma((devices, HALVES)), dma, dma,
        ],
        compiler_params=pltpu.CompilerParams(
            collective_id=0, has_side_effects=True, vmem_limit_bytes=40 * 1024 * 1024),
        name="gather_rows",
    )(hidden, norm_gain.reshape(1, width), jnp.swapaxes(token_ids, 1, 2))
    logits = lax.dot_general(
        lm_head, rows.reshape(total, width), (((1,), (1,)), ((), ())), preferred_element_type=jnp.float32)
    vocab_start = (lax.axis_index("dec") * tp_n + lax.axis_index("tp")) * vocab
    seg_ids = doc_ids[:, 0, :doc_rows].reshape(1, total)
    peak = jnp.max(logits, axis=0, keepdims=True)
    summed = jnp.sum(jnp.exp(logits - peak), axis=0, keepdims=True)
    entry = (vocab_start + jnp.arange(vocab, dtype=jnp.int32)).astype(jnp.float32)
    target = jnp.sum(jnp.where(entry[:, None] == seg_ids, logits, 0.0), axis=0, keepdims=True)
    stats = jnp.concatenate([peak, summed, target], axis=0).reshape(3, dec_n, doc_rows)
    stats = jnp.pad(jnp.swapaxes(stats, 0, 1), ((0, 0), (0, 5), (0, 128 - doc_rows)))
    return pl.pallas_call(
        functools.partial(exchange_kernel, dec_n, tp_n, length, slots),
        out_shape=(out, out),
        in_specs=[vmem, pl.BlockSpec(memory_space=pltpu.SMEM)],
        out_specs=(vmem, vmem),
        scratch_shapes=[
            pltpu.VMEM((dec_n, 8, 128), jnp.float32),
            pltpu.VMEM((8, 128), jnp.float32),
            pltpu.VMEM((tp_n, 8, 128), jnp.float32),
            dma, dma, dma, dma,
        ],
        compiler_params=pltpu.CompilerParams(
            collective_id=1, has_side_effects=True, vmem_limit_bytes=16 * 1024 * 1024),
        name="exchange_parts",
    )(stats, doc_counts)


def solution(mesh):
    placed = (
        P("dec", "tp", None, None),
        P(),
        P(("dec", "tp"), None),
        P("dec", None, None),
        P("dec"),
    )
    return jax.shard_map(
        functools.partial(body, mesh.shape["dec"], mesh.shape["tp"]),
        mesh=mesh,
        in_specs=placed,
        out_specs=(P("dec", "tp"), P("dec", "tp")),
        check_vma=False,
    )
```

```python
import functools

import jax
import jax.numpy as jnp
from jax import lax
from jax.experimental import pallas as pl
from jax.experimental.pallas import tpu as pltpu
from jax.sharding import PartitionSpec as P

MESH = pl.DeviceIdType.MESH
CORES = 2
HALVES = 2
EPS = 1e-05


def flip(index, mask):
    bit = 1
    while bit <= mask:
        if mask & bit:
            index = index + bit - 2 * bit * ((index // bit) % 2)
        bit *= 2
    return index


def kernel(dec_n, tp_n, hidden_hbm, gain_hbm, lm_head, ids_hbm, counts, hyp_ref, post_ref,
           hidden, gain, ids, weights, rows, doc_ids, id_row, fresh, logits, stat_row, stats, got_dec, stat_doc, got_tp,
           h_sem, g_sem, i_sem, w_sem, z_send, z_recv, u_send, u_recv, v_send, v_recv,
           uv_send, uv_recv, vu_send, vu_recv, mate_send, mate_recv, id_send, id_recv, dec_send, dec_recv, tp_send, tp_recv):
    slots, length, width = hidden.shape[1:]
    own_rows = slots * length
    doc_rows = tp_n * own_rows
    vocab = lm_head.shape[0]
    z_n = dec_n // CORES
    x_n = 2 ** ((tp_n.bit_length()) // 2)
    assert x_n * x_n == tp_n
    half = width // HALVES
    piece_width = half // HALVES
    z_half = z_n // 2
    dec, tp = lax.axis_index("dec"), lax.axis_index("tp")
    z, core = dec // CORES, dec % CORES
    u_step = 1 + core * (x_n - 1)
    v_step = x_n - core * (x_n - 1)
    u, v = (tp // u_step) % x_n, (tp // v_step) % x_n

    barrier = pltpu.get_barrier_semaphore()
    for d in range(1, dec_n):
        pl.semaphore_signal(barrier, inc=1, device_id=(flip(dec, d), tp), device_id_type=MESH)
    for d in range(1, tp_n):
        pl.semaphore_signal(barrier, inc=1, device_id=(dec, flip(tp, d)), device_id_type=MESH)
    loads = [pltpu.make_async_copy(*pair) for pair in (
        (hidden_hbm, hidden, h_sem), (gain_hbm, gain, g_sem), (ids_hbm, ids, i_sem), (lm_head, weights, w_sem))]
    for load in loads:
        load.start()
    for load in loads[:3]:
        load.wait()

    for s in range(slots):
        part = hidden[0, s]
        meansq = jnp.mean(part * part, axis=1, keepdims=True)
        fresh[s * length:(s + 1) * length, :] = part * lax.rsqrt(meansq + EPS) * gain[...]
    rows[z, core, tp] = jnp.concatenate(
        [fresh[:, 0:half], fresh[:, half:width]], axis=0).astype(jnp.bfloat16)

    all_slots = ids.shape[2]
    lane = lax.broadcasted_iota(jnp.int32, (length, 128), 1)
    token = lax.broadcasted_iota(jnp.int32, (length, 128), 0)
    values = ids[0].astype(jnp.float32)
    spread = jnp.zeros((length, 128), jnp.float32)
    for s in range(all_slots):
        spread = jnp.where(lane == s * length + token, values[:, s:s + 1], spread)
    doc_ids[dec] = jnp.broadcast_to(jnp.sum(spread, axis=0, keepdims=True), doc_ids.shape[1:])
    stats[...] = jnp.zeros_like(stats)
    stat_doc[...] = jnp.zeros_like(stat_doc)

    pl.semaphore_wait(barrier, dec_n + tp_n - 2)

    def place(vv, uu):
        return vv * v_step + uu * u_step

    def send(piece, send_sem, recv_sem, to_dec, to_tp):
        pltpu.make_async_remote_copy(
            src_ref=piece, dst_ref=piece, send_sem=send_sem, recv_sem=recv_sem,
            device_id=(to_dec, to_tp), device_id_type=MESH).start()

    def wait(piece, sem):
        pltpu.make_async_copy(piece, piece, sem).wait()

    first_z = (z // z_half) * z_half
    groups = [pl.ds(first_z, z_half), pl.ds(z_half - first_z, z_half)]
    low, high = pl.ds(0, piece_width), pl.ds(piece_width, piece_width)
    near = range(1, x_n)

    for d in range(1, z_n):
        send(rows.at[z, core, tp], z_send, z_recv.at[d // z_half], flip(z, d) * CORES + core, tp)
    for d in range(1, dec_n):
        send(doc_ids.at[dec], id_send, id_recv, flip(dec, d), tp)
    for g, group in enumerate(groups):
        wait(rows.at[pl.ds(0, z_half - 1 + g), core, tp], z_recv.at[g])
        column = rows.at[group, core, tp]
        for e in near:
            send(column, u_send, u_recv.at[g, e], dec, place(v, flip(u, e)))
            send(column, v_send, v_recv.at[g, e], dec, place(flip(v, e), u))
    for g, group in enumerate(groups):
        for e in near:
            at = place(v, flip(u, e))
            wait(rows.at[group, core, at], u_recv.at[g, e])
            for f in near:
                send(rows.at[group, core, at, :, low], uv_send, uv_recv.at[g, e, f], dec, place(flip(v, f), u))
            at = place(flip(v, e), u)
            wait(rows.at[group, core, at], v_recv.at[g, e])
            for f in near:
                send(rows.at[group, core, at, :, high], vu_send, vu_recv.at[g, f, e], dec, place(v, flip(u, f)))
    for g, group in enumerate(groups):
        for e in near:
            for f in near:
                at = place(flip(v, f), flip(u, e))
                wait(rows.at[group, core, at, :, low], uv_recv.at[g, e, f])
                wait(rows.at[group, core, at, :, high], vu_recv.at[g, e, f])
        send(rows.at[group, core], mate_send, mate_recv.at[g], flip(dec, 1), tp)
    others = pltpu.make_async_copy(doc_ids.at[0:dec_n - 1], doc_ids.at[0:dec_n - 1], id_recv)
    others.wait()
    loads[3].wait()
    for g, group in enumerate(groups):
        wait(rows.at[group, 1 - core], mate_recv.at[g])

    for g in range(dec_n):
        id_row[0:1, g * doc_rows:(g + 1) * doc_rows] = doc_ids[g, 0:1, 0:doc_rows]

    total = dec_n * doc_rows
    decs = max(1, min(256, total) // doc_rows)
    tile = decs * doc_rows
    step = 512
    flat = rows.reshape(dec_n, tp_n, HALVES * own_rows, half)
    vocab_start = (dec * tp_n + tp) * vocab

    @pl.loop(0, total // tile)
    def _(t):
        logits[...] = jnp.zeros((vocab, tile), jnp.float32)

        @pl.loop(0, half // step)
        def _(k):
            at = pl.ds(pl.multiple_of(k * step, step), step)
            beyond = pl.ds(pl.multiple_of(k * step + half, step), step)
            both = flat[pl.ds(t * decs, decs), :, :, at].astype(jnp.float32)
            for side, columns in enumerate((at, beyond)):
                some = both[:, :, side * own_rows:(side + 1) * own_rows].reshape(tile, step)
                logits[...] += lax.dot_general(
                    weights[:, columns], some.astype(jnp.bfloat16), (((1,), (1,)), ((), ())),
                    preferred_element_type=jnp.float32)

        value = logits[...]
        peak = jnp.max(value, axis=0, keepdims=True)
        place = pl.ds(pl.multiple_of(t * tile, tile), tile)
        entry = (lax.broadcasted_iota(jnp.int32, (vocab, tile), 0) + vocab_start).astype(jnp.float32)
        stat_row[0:1, place] = peak
        stat_row[1:2, place] = jnp.sum(jnp.exp(value - peak), axis=0, keepdims=True)
        stat_row[2:3, place] = jnp.sum(
            jnp.where(entry == id_row[0:1, place], value, 0.0), axis=0, keepdims=True)

    for g in range(dec_n):
        stats[g, 0:3, 0:doc_rows] = stat_row[0:3, g * doc_rows:(g + 1) * doc_rows]
    got_dec[dec] = stats[dec]
    for d in range(1, dec_n):
        to = flip(dec, d)
        pltpu.make_async_remote_copy(
            src_ref=stats.at[to], dst_ref=got_dec.at[dec], send_sem=dec_send,
            recv_sem=dec_recv, device_id=(to, tp), device_id_type=MESH).start()
    come = pltpu.make_async_copy(got_dec.at[0:dec_n - 1], got_dec.at[0:dec_n - 1], dec_recv)
    come.wait()

    def merged(got):
        peak = jnp.max(got[:, 0:1, :], axis=0)
        summed = jnp.sum(got[:, 1:2, :] * jnp.exp(got[:, 0:1, :] - peak[None]), axis=0)
        return peak, summed, jnp.sum(got[:, 2:3, :], axis=0)

    for i, value in enumerate(merged(got_dec[...])):
        stat_doc[i:i + 1, :] = value
    got_tp[tp] = stat_doc[...]
    for d in range(1, tp_n):
        pltpu.make_async_remote_copy(
            src_ref=stat_doc, dst_ref=got_tp.at[tp], send_sem=tp_send,
            recv_sem=tp_recv, device_id=(dec, flip(tp, d)), device_id_type=MESH).start()
    pltpu.make_async_copy(got_tp.at[0:tp_n - 1], got_tp.at[0:tp_n - 1], tp_recv).wait()
    peak, summed, target = merged(got_tp[...])

    logp = target - (peak + jnp.log(summed))
    score = logp
    for l in range(1, length):
        score = score + pltpu.roll(logp, 128 - l, 1)
    score = score / length
    lane = lax.broadcasted_iota(jnp.int32, (1, 128), 1)
    first = jnp.logical_and(lane % length == 0, lane < doc_rows)
    alive = jnp.logical_and(first, lane // length < counts[0])
    best = jnp.max(jnp.where(alive, score, -jnp.inf), axis=1, keepdims=True)
    norm = best + jnp.log(jnp.sum(
        jnp.exp(jnp.where(alive, score - best, -jnp.inf)), axis=1, keepdims=True))
    hyp = jnp.where(alive, score, 0.0)
    post = jnp.where(alive, score - norm, 0.0)
    out_lane = lax.broadcasted_iota(jnp.int32, (1, slots), 1)
    hyp_out = jnp.zeros((1, slots), jnp.float32)
    post_out = jnp.zeros((1, slots), jnp.float32)
    for s in range(slots):
        here = lane == (tp * slots + s) * length
        hyp_out = jnp.where(out_lane == s, jnp.sum(jnp.where(here, hyp, 0.0), axis=1, keepdims=True), hyp_out)
        post_out = jnp.where(out_lane == s, jnp.sum(jnp.where(here, post, 0.0), axis=1, keepdims=True), post_out)
    hyp_ref[...] = hyp_out
    post_ref[...] = post_out

    wait(rows.at[0:z_n - 1, 0, 0], z_send)
    for sem in (u_send, v_send):
        wait(rows.at[:, 0, 0:x_n - 1], sem)
    for sem in (uv_send, vu_send):
        wait(rows.at[:, 0, 0:(x_n - 1) ** 2, :, low], sem)
    wait(rows.at[:, 0], mate_send)
    pltpu.make_async_copy(doc_ids.at[0:dec_n - 1], doc_ids.at[0:dec_n - 1], id_send).wait()
    pltpu.make_async_copy(got_dec.at[0:dec_n - 1], got_dec.at[0:dec_n - 1], dec_send).wait()
    pltpu.make_async_copy(got_tp.at[0:tp_n - 1], got_tp.at[0:tp_n - 1], tp_send).wait()


def body(dec_n, tp_n, hidden, norm_gain, lm_head, token_ids, doc_counts):
    slots, length, width = hidden.shape[1:]
    own_rows = slots * length
    devices = dec_n * tp_n
    vocab = lm_head.shape[0]
    total = devices * own_rows
    all_slots = token_ids.shape[1]
    vmem = pl.BlockSpec(memory_space=pltpu.VMEM)
    out = jax.ShapeDtypeStruct((1, slots), jnp.float32)
    dma = pltpu.SemaphoreType.DMA
    side = 2 ** (tp_n.bit_length() // 2)
    return pl.pallas_call(
        functools.partial(kernel, dec_n, tp_n),
        out_shape=(out, out),
        in_specs=[pl.BlockSpec(memory_space=pl.ANY)] * 4 + [pl.BlockSpec(memory_space=pltpu.SMEM)],
        out_specs=(vmem, vmem),
        scratch_shapes=[
            pltpu.VMEM(hidden.shape, jnp.float32),
            pltpu.VMEM((1, width), jnp.float32),
            pltpu.VMEM((1, length, all_slots), jnp.int32),
            pltpu.VMEM((vocab, width), jnp.bfloat16),
            pltpu.VMEM((dec_n // CORES, CORES, tp_n, HALVES * own_rows, width // HALVES), jnp.bfloat16),
            pltpu.VMEM((dec_n, 8, 128), jnp.float32),
            pltpu.VMEM((8, total), jnp.float32),
            pltpu.VMEM((own_rows, width), jnp.float32),
            pltpu.VMEM((vocab, min(256, total)), jnp.float32),
            pltpu.VMEM((8, total), jnp.float32),
            pltpu.VMEM((dec_n, 8, 128), jnp.float32),
            pltpu.VMEM((dec_n, 8, 128), jnp.float32),
            pltpu.VMEM((8, 128), jnp.float32),
            pltpu.VMEM((tp_n, 8, 128), jnp.float32),
            dma, dma, dma, dma, dma, dma((2,)), dma, dma((2, side)), dma, dma((2, side)),
            dma, dma((2, side, side)), dma, dma((2, side, side)), dma, dma((2,)),
            dma, dma, dma, dma, dma, dma,
        ],
        compiler_params=pltpu.CompilerParams(
            collective_id=0, has_side_effects=True, vmem_limit_bytes=60 * 1024 * 1024),
        name="rescore",
    )(hidden, norm_gain.reshape(1, width), lm_head, jnp.swapaxes(token_ids, 1, 2), doc_counts)


def solution(mesh):
    placed = (
        P("dec", "tp", None, None),
        P(),
        P(("dec", "tp"), None),
        P("dec", None, None),
        P("dec"),
    )
    return jax.shard_map(
        functools.partial(body, mesh.shape["dec"], mesh.shape["tp"]),
        mesh=mesh,
        in_specs=placed,
        out_specs=(P("dec", "tp"), P("dec", "tp")),
        check_vma=False,
    )
```

```python
import functools

import jax
import jax.numpy as jnp
from jax import lax
from jax.experimental import pallas as pl
from jax.experimental.pallas import tpu as pltpu
from jax.sharding import PartitionSpec as P

MESH = pl.DeviceIdType.MESH
CORES = 2
HALVES = 2
ID_LANES = 128
EPS = 1e-05


def flip(index, mask):
    bit = 1
    while bit <= mask:
        if mask & bit:
            index = index + bit - 2 * bit * ((index // bit) % 2)
        bit *= 2
    return index


def kernel(dec_n, tp_n, hidden_hbm, gain_hbm, lm_head, ids_hbm, counts, hyp_ref, post_ref,
           hidden, gain, ids, weights, rows, fresh, logits, stats, got_dec, stat_doc, got_tp,
           h_sem, g_sem, i_sem, w_sem, z_send, z_recv, u_send, u_recv, v_send, v_recv,
           uv_send, uv_recv, vu_send, vu_recv, mate_send, mate_recv, dec_send, dec_recv, tp_send, tp_recv):
    slots, length, width = hidden.shape[1:]
    own_rows = slots * length
    doc_rows = tp_n * own_rows
    vocab = lm_head.shape[0]
    z_n = dec_n // CORES
    x_n = 2 ** ((tp_n.bit_length()) // 2)
    assert x_n * x_n == tp_n
    half = width // HALVES
    piece_width = half // HALVES
    z_half = z_n // 2
    dec, tp = lax.axis_index("dec"), lax.axis_index("tp")
    z, core = dec // CORES, dec % CORES
    u_step = 1 + core * (x_n - 1)
    v_step = x_n - core * (x_n - 1)
    u, v = (tp // u_step) % x_n, (tp // v_step) % x_n

    barrier = pltpu.get_barrier_semaphore()
    for d in range(1, dec_n):
        pl.semaphore_signal(barrier, inc=1, device_id=(flip(dec, d), tp), device_id_type=MESH)
    for d in range(1, tp_n):
        pl.semaphore_signal(barrier, inc=1, device_id=(dec, flip(tp, d)), device_id_type=MESH)
    loads = [pltpu.make_async_copy(*pair) for pair in (
        (hidden_hbm, hidden, h_sem), (gain_hbm, gain, g_sem), (ids_hbm, ids, i_sem), (lm_head, weights, w_sem))]
    for load in loads:
        load.start()
    for load in loads[:3]:
        load.wait()

    for s in range(slots):
        part = hidden[0, s]
        meansq = jnp.mean(part * part, axis=1, keepdims=True)
        fresh[s * length:(s + 1) * length, :] = part * lax.rsqrt(meansq + EPS) * gain[...]
    rows[z, core, tp, :, 0:half] = jnp.concatenate(
        [fresh[:, 0:half], fresh[:, half:width]], axis=0).astype(jnp.bfloat16)

    lane = lax.broadcasted_iota(jnp.int32, (length, ID_LANES), 1)
    slot = lax.broadcasted_iota(jnp.int32, ids.shape[1:], 1)
    digits = []
    for s in range(slots):
        here = jnp.where(slot == tp * slots + s, ids[0], 0).astype(jnp.float32)
        token = jnp.sum(here, axis=1, keepdims=True).astype(jnp.int32)
        shift = jnp.where(lane == 0, 12, jnp.where(lane == 1, 6, 0))
        digit = jnp.bitwise_and(jnp.right_shift(jnp.broadcast_to(token, lane.shape), shift), 63)
        digits.append(jnp.where(lane < 3, digit, 0).astype(jnp.float32))
    digits.append(jnp.zeros((own_rows, ID_LANES), jnp.float32))
    rows[z, core, tp, :, half:half + ID_LANES] = jnp.concatenate(digits, axis=0).astype(jnp.bfloat16)
    stats[...] = jnp.zeros_like(stats)
    stat_doc[...] = jnp.zeros_like(stat_doc)

    pl.semaphore_wait(barrier, dec_n + tp_n - 2)

    def place(vv, uu):
        return vv * v_step + uu * u_step

    def send(piece, send_sem, recv_sem, to_dec, to_tp):
        pltpu.make_async_remote_copy(
            src_ref=piece, dst_ref=piece, send_sem=send_sem, recv_sem=recv_sem,
            device_id=(to_dec, to_tp), device_id_type=MESH).start()

    def wait(piece, sem):
        pltpu.make_async_copy(piece, piece, sem).wait()

    first_z = (z // z_half) * z_half
    groups = [pl.ds(first_z, z_half), pl.ds(z_half - first_z, z_half)]
    low, high = pl.ds(0, piece_width), pl.ds(piece_width, piece_width + ID_LANES)
    near = range(1, x_n)

    for d in range(1, z_n):
        send(rows.at[z, core, tp], z_send, z_recv.at[d // z_half], flip(z, d) * CORES + core, tp)
    for g, group in enumerate(groups):
        wait(rows.at[pl.ds(0, z_half - 1 + g), core, tp], z_recv.at[g])
        column = rows.at[group, core, tp]
        for e in near:
            send(column, u_send, u_recv.at[g, e], dec, place(v, flip(u, e)))
            send(column, v_send, v_recv.at[g, e], dec, place(flip(v, e), u))
    for g, group in enumerate(groups):
        for e in near:
            at = place(v, flip(u, e))
            wait(rows.at[group, core, at], u_recv.at[g, e])
            for f in near:
                send(rows.at[group, core, at, :, low], uv_send, uv_recv.at[g, e, f], dec, place(flip(v, f), u))
            at = place(flip(v, e), u)
            wait(rows.at[group, core, at], v_recv.at[g, e])
            for f in near:
                send(rows.at[group, core, at, :, high], vu_send, vu_recv.at[g, f, e], dec, place(v, flip(u, f)))
    for g, group in enumerate(groups):
        for e in near:
            for f in near:
                at = place(flip(v, f), flip(u, e))
                wait(rows.at[group, core, at, :, low], uv_recv.at[g, e, f])
                wait(rows.at[group, core, at, :, high], vu_recv.at[g, e, f])
        send(rows.at[group, core], mate_send, mate_recv.at[g], flip(dec, 1), tp)
    loads[3].wait()

    z_some = max(1, min(256, z_n * doc_rows) // doc_rows)
    tile = z_some * doc_rows
    step = 512
    vocab_start = (dec * tp_n + tp) * vocab
    column = lax.broadcasted_iota(jnp.int32, (8, ID_LANES), 1)
    scale = jnp.where(column == 0, 4096.0, jnp.where(column == 1, 64.0, jnp.where(column == 2, 1.0, 0.0)))

    def times_rows(left, right):
        return lax.dot_general(left, right.reshape(tile, right.shape[-1]).astype(jnp.bfloat16),
                               (((1,), (1,)), ((), ())), preferred_element_type=jnp.float32)

    def score_rows(which):
        @pl.loop(0, z_n // z_some)
        def _(t):
            logits[...] = jnp.zeros((vocab, tile), jnp.float32)
            some = pl.ds(t * z_some, z_some)

            @pl.loop(0, half // step)
            def _(k):
                at = pl.ds(pl.multiple_of(k * step, step), step)
                beyond = pl.ds(pl.multiple_of(k * step + half, step), step)
                both = rows[some, which, :, :, at].astype(jnp.float32)
                logits[...] += (times_rows(weights[:, at], both[:, :, 0:own_rows])
                                + times_rows(weights[:, beyond], both[:, :, own_rows:2 * own_rows]))

            tail = rows[some, which, :, :, pl.ds(half, ID_LANES)].astype(jnp.float32)
            row_ids = times_rows(scale.astype(jnp.bfloat16), tail[:, :, 0:own_rows])[0:1, :]
            value = logits[...]
            peak = jnp.max(value, axis=0, keepdims=True)
            summed = jnp.sum(jnp.exp(value - peak), axis=0, keepdims=True)
            entry = (lax.broadcasted_iota(jnp.int32, (vocab, tile), 0) + vocab_start).astype(jnp.float32)
            target = jnp.sum(jnp.where(entry == row_ids, value, 0.0), axis=0, keepdims=True)
            for i in range(z_some):
                for j, stat in enumerate((peak, summed, target)):
                    stats[(t * z_some + i) * CORES + which, j:j + 1, 0:doc_rows] = stat[:, i * doc_rows:(i + 1) * doc_rows]

    score_rows(core)
    for g, group in enumerate(groups):
        wait(rows.at[group, 1 - core], mate_recv.at[g])
    score_rows(1 - core)

    got_dec[dec] = stats[dec]
    for d in range(1, dec_n):
        to = flip(dec, d)
        pltpu.make_async_remote_copy(
            src_ref=stats.at[to], dst_ref=got_dec.at[dec], send_sem=dec_send,
            recv_sem=dec_recv, device_id=(to, tp), device_id_type=MESH).start()
    come = pltpu.make_async_copy(got_dec.at[0:dec_n - 1], got_dec.at[0:dec_n - 1], dec_recv)
    come.wait()

    def merged(got):
        peak = jnp.max(got[:, 0:1, :], axis=0)
        summed = jnp.sum(got[:, 1:2, :] * jnp.exp(got[:, 0:1, :] - peak[None]), axis=0)
        return peak, summed, jnp.sum(got[:, 2:3, :], axis=0)

    for i, value in enumerate(merged(got_dec[...])):
        stat_doc[i:i + 1, :] = value
    got_tp[tp] = stat_doc[...]
    for d in range(1, tp_n):
        pltpu.make_async_remote_copy(
            src_ref=stat_doc, dst_ref=got_tp.at[tp], send_sem=tp_send,
            recv_sem=tp_recv, device_id=(dec, flip(tp, d)), device_id_type=MESH).start()
    pltpu.make_async_copy(got_tp.at[0:tp_n - 1], got_tp.at[0:tp_n - 1], tp_recv).wait()
    peak, summed, target = merged(got_tp[...])

    logp = target - (peak + jnp.log(summed))
    score = logp
    for l in range(1, length):
        score = score + pltpu.roll(logp, 128 - l, 1)
    score = score / length
    lane = lax.broadcasted_iota(jnp.int32, (1, 128), 1)
    first = jnp.logical_and(lane % length == 0, lane < doc_rows)
    alive = jnp.logical_and(first, lane // length < counts[0])
    best = jnp.max(jnp.where(alive, score, -jnp.inf), axis=1, keepdims=True)
    norm = best + jnp.log(jnp.sum(
        jnp.exp(jnp.where(alive, score - best, -jnp.inf)), axis=1, keepdims=True))
    hyp = jnp.where(alive, score, 0.0)
    post = jnp.where(alive, score - norm, 0.0)
    out_lane = lax.broadcasted_iota(jnp.int32, (1, slots), 1)
    hyp_out = jnp.zeros((1, slots), jnp.float32)
    post_out = jnp.zeros((1, slots), jnp.float32)
    for s in range(slots):
        here = lane == (tp * slots + s) * length
        hyp_out = jnp.where(out_lane == s, jnp.sum(jnp.where(here, hyp, 0.0), axis=1, keepdims=True), hyp_out)
        post_out = jnp.where(out_lane == s, jnp.sum(jnp.where(here, post, 0.0), axis=1, keepdims=True), post_out)
    hyp_ref[...] = hyp_out
    post_ref[...] = post_out

    wait(rows.at[0:z_n - 1, 0, 0], z_send)
    for sem in (u_send, v_send):
        wait(rows.at[:, 0, 0:x_n - 1], sem)
    for sem, piece in ((uv_send, low), (vu_send, high)):
        wait(rows.at[:, 0, 0:(x_n - 1) ** 2, :, piece], sem)
    wait(rows.at[:, 0], mate_send)
    pltpu.make_async_copy(got_dec.at[0:dec_n - 1], got_dec.at[0:dec_n - 1], dec_send).wait()
    pltpu.make_async_copy(got_tp.at[0:tp_n - 1], got_tp.at[0:tp_n - 1], tp_send).wait()


def body(dec_n, tp_n, hidden, norm_gain, lm_head, token_ids, doc_counts):
    slots, length, width = hidden.shape[1:]
    own_rows = slots * length
    vocab = lm_head.shape[0]
    doc_rows = tp_n * own_rows
    z_some = max(1, min(256, dec_n // CORES * doc_rows) // doc_rows)
    all_slots = token_ids.shape[1]
    vmem = pl.BlockSpec(memory_space=pltpu.VMEM)
    out = jax.ShapeDtypeStruct((1, slots), jnp.float32)
    dma = pltpu.SemaphoreType.DMA
    side = 2 ** (tp_n.bit_length() // 2)
    return pl.pallas_call(
        functools.partial(kernel, dec_n, tp_n),
        out_shape=(out, out),
        in_specs=[pl.BlockSpec(memory_space=pl.ANY)] * 4 + [pl.BlockSpec(memory_space=pltpu.SMEM)],
        out_specs=(vmem, vmem),
        scratch_shapes=[
            pltpu.VMEM(hidden.shape, jnp.float32),
            pltpu.VMEM((1, width), jnp.float32),
            pltpu.VMEM((1, length, all_slots), jnp.int32),
            pltpu.VMEM((vocab, width), jnp.bfloat16),
            pltpu.VMEM((dec_n // CORES, CORES, tp_n, HALVES * own_rows, width // HALVES + ID_LANES), jnp.bfloat16),
            pltpu.VMEM((own_rows, width), jnp.float32),
            pltpu.VMEM((vocab, z_some * doc_rows), jnp.float32),
            pltpu.VMEM((dec_n, 8, 128), jnp.float32),
            pltpu.VMEM((dec_n, 8, 128), jnp.float32),
            pltpu.VMEM((8, 128), jnp.float32),
            pltpu.VMEM((tp_n, 8, 128), jnp.float32),
            dma, dma, dma, dma, dma, dma((2,)), dma, dma((2, side)), dma, dma((2, side)),
            dma, dma((2, side, side)), dma, dma((2, side, side)), dma, dma((2,)),
            dma, dma, dma, dma,
        ],
        compiler_params=pltpu.CompilerParams(
            collective_id=0, has_side_effects=True, vmem_limit_bytes=60 * 1024 * 1024),
        name="rescore",
    )(hidden, norm_gain.reshape(1, width), lm_head, jnp.swapaxes(token_ids, 1, 2), doc_counts)


def solution(mesh):
    placed = (
        P("dec", "tp", None, None),
        P(),
        P(("dec", "tp"), None),
        P("dec", None, None),
        P("dec"),
    )
    return jax.shard_map(
        functools.partial(body, mesh.shape["dec"], mesh.shape["tp"]),
        mesh=mesh,
        in_specs=placed,
        out_specs=(P("dec", "tp"), P("dec", "tp")),
        check_vma=False,
    )
```

```python
import functools

import jax
import jax.numpy as jnp
from jax import lax
from jax.experimental import pallas as pl
from jax.experimental.pallas import tpu as pltpu
from jax.sharding import PartitionSpec as P

MESH = pl.DeviceIdType.MESH
CORES = 2
HALVES = 2
ID_LANES = 128
EPS = 1e-05


def flip(index, mask):
    bit = 1
    while bit <= mask:
        if mask & bit:
            index = index + bit - 2 * bit * ((index // bit) % 2)
        bit *= 2
    return index


def kernel(dec_n, tp_n, hidden_hbm, gain_hbm, lm_head, ids_hbm, counts, hyp_ref, post_ref,
           hidden, gain, ids, weights, rows, fresh, logits, stats, got_dec, stat_doc, got_tp,
           h_sem, g_sem, i_sem, w_sem, z_send, z_recv, u_send, u_recv, v_send, v_recv,
           uv_send, uv_recv, vu_send, vu_recv, mate_send, mate_recv, dec_send, dec_recv, tp_send, tp_recv):
    slots, length, width = hidden.shape[1:]
    own_rows = slots * length
    doc_rows = tp_n * own_rows
    vocab = lm_head.shape[0]
    z_n = dec_n // CORES
    x_n = 2 ** ((tp_n.bit_length()) // 2)
    assert x_n * x_n == tp_n
    half = width // HALVES
    piece_width = half // HALVES
    z_half = z_n // 2
    dec, tp = lax.axis_index("dec"), lax.axis_index("tp")
    z, core = dec // CORES, dec % CORES
    u_step = 1 + core * (x_n - 1)
    v_step = x_n - core * (x_n - 1)
    u, v = (tp // u_step) % x_n, (tp // v_step) % x_n

    loads = [pltpu.make_async_copy(*pair) for pair in (
        (hidden_hbm, hidden, h_sem), (gain_hbm, gain, g_sem), (ids_hbm, ids, i_sem), (lm_head, weights, w_sem))]
    for load in loads:
        load.start()
    barrier = pltpu.get_barrier_semaphore()
    for d in range(1, dec_n):
        pl.semaphore_signal(barrier, inc=1, device_id=(flip(dec, d), tp), device_id_type=MESH)
    for d in range(1, tp_n):
        pl.semaphore_signal(barrier, inc=1, device_id=(dec, flip(tp, d)), device_id_type=MESH)
    for load in loads[:3]:
        load.wait()

    for s in range(slots):
        part = hidden[0, s]
        meansq = jnp.mean(part * part, axis=1, keepdims=True)
        fresh[s * length:(s + 1) * length, :] = part * lax.rsqrt(meansq + EPS) * gain[...]
    rows[z, core, tp, :, 0:half] = jnp.concatenate(
        [fresh[:, 0:half], fresh[:, half:width]], axis=0).astype(jnp.bfloat16)

    lane = lax.broadcasted_iota(jnp.int32, (length, ID_LANES), 1)
    slot = lax.broadcasted_iota(jnp.int32, ids.shape[1:], 1)
    digits = []
    for s in range(slots):
        here = jnp.where(slot == tp * slots + s, ids[0], 0).astype(jnp.float32)
        token = jnp.sum(here, axis=1, keepdims=True).astype(jnp.int32)
        shift = jnp.where(lane == 0, 12, jnp.where(lane == 1, 6, 0))
        digit = jnp.bitwise_and(jnp.right_shift(jnp.broadcast_to(token, lane.shape), shift), 63)
        digits.append(jnp.where(lane < 3, digit, 0).astype(jnp.float32))
    digits.append(jnp.zeros((own_rows, ID_LANES), jnp.float32))
    rows[z, core, tp, :, half:half + ID_LANES] = jnp.concatenate(digits, axis=0).astype(jnp.bfloat16)
    stats[...] = jnp.zeros_like(stats)
    stat_doc[...] = jnp.zeros_like(stat_doc)

    pl.semaphore_wait(barrier, dec_n + tp_n - 2)

    def place(vv, uu):
        return vv * v_step + uu * u_step

    def send(piece, send_sem, recv_sem, to_dec, to_tp):
        pltpu.make_async_remote_copy(
            src_ref=piece, dst_ref=piece, send_sem=send_sem, recv_sem=recv_sem,
            device_id=(to_dec, to_tp), device_id_type=MESH).start()

    def wait(piece, sem):
        pltpu.make_async_copy(piece, piece, sem).wait()

    first_z = (z // z_half) * z_half
    groups = [pl.ds(first_z, z_half), pl.ds(z_half - first_z, z_half)]
    low, high = pl.ds(0, piece_width), pl.ds(piece_width, piece_width + ID_LANES)
    near = range(1, x_n)

    for d in range(1, z_n):
        send(rows.at[z, core, tp], z_send, z_recv.at[d // z_half], flip(z, d) * CORES + core, tp)
    for g, group in enumerate(groups):
        wait(rows.at[pl.ds(0, z_half - 1 + g), core, tp], z_recv.at[g])
        column = rows.at[group, core, tp]
        for e in near:
            send(column, u_send, u_recv.at[g, e], dec, place(v, flip(u, e)))
            send(column, v_send, v_recv.at[g, e], dec, place(flip(v, e), u))
    for g, group in enumerate(groups):
        for e in near:
            at = place(v, flip(u, e))
            wait(rows.at[group, core, at], u_recv.at[g, e])
            for f in near:
                send(rows.at[group, core, at, :, low], uv_send, uv_recv.at[g, e, f], dec, place(flip(v, f), u))
            at = place(flip(v, e), u)
            wait(rows.at[group, core, at], v_recv.at[g, e])
            for f in near:
                send(rows.at[group, core, at, :, high], vu_send, vu_recv.at[g, f, e], dec, place(v, flip(u, f)))
    for g, group in enumerate(groups):
        for e in near:
            for f in near:
                at = place(flip(v, f), flip(u, e))
                wait(rows.at[group, core, at, :, low], uv_recv.at[g, e, f])
                wait(rows.at[group, core, at, :, high], vu_recv.at[g, e, f])
        send(rows.at[group, core], mate_send, mate_recv.at[g], flip(dec, 1), tp)
    loads[3].wait()

    decs = max(1, min(256, dec_n * doc_rows) // doc_rows)
    tile = decs * doc_rows
    step = 1024
    flat = rows.reshape(dec_n, tp_n, 2 * own_rows, half + ID_LANES)
    vocab_start = (dec * tp_n + tp) * vocab
    column = lax.broadcasted_iota(jnp.int32, (8, ID_LANES), 1)
    scale = jnp.where(column == 0, 4096.0, jnp.where(column == 1, 64.0, jnp.where(column == 2, 1.0, 0.0)))

    def times_rows(left, right):
        return lax.dot_general(left, right.reshape(tile, right.shape[-1]).astype(jnp.bfloat16),
                               (((1,), (1,)), ((), ())), preferred_element_type=jnp.float32)

    for g, group in enumerate(groups):
        wait(rows.at[group, 1 - core], mate_recv.at[g])

    @pl.loop(0, dec_n // decs)
    def _(t):
        logits[...] = jnp.zeros((vocab, tile), jnp.float32)
        some = pl.ds(t * decs, decs)

        @pl.loop(0, half // step)
        def _(k):
            at = pl.ds(pl.multiple_of(k * step, step), step)
            beyond = pl.ds(pl.multiple_of(k * step + half, step), step)
            both = flat[some, :, :, at].astype(jnp.float32)
            logits[...] += (times_rows(weights[:, at], both[:, :, 0:own_rows])
                            + times_rows(weights[:, beyond], both[:, :, own_rows:2 * own_rows]))

        tail = flat[some, :, :, pl.ds(half, ID_LANES)].astype(jnp.float32)
        row_ids = times_rows(scale.astype(jnp.bfloat16), tail[:, :, 0:own_rows])[0:1, :]
        value = logits[...]
        peak = jnp.max(value, axis=0, keepdims=True)
        summed = jnp.sum(jnp.exp(value - peak), axis=0, keepdims=True)
        entry = (lax.broadcasted_iota(jnp.int32, (vocab, tile), 0) + vocab_start).astype(jnp.float32)
        target = jnp.sum(jnp.where(entry == row_ids, value, 0.0), axis=0, keepdims=True)
        which = lax.broadcasted_iota(jnp.int32, (8, tile), 0)
        stat = jnp.where(which == 0, peak, jnp.where(which == 1, summed, target))
        for i in range(decs):
            stats[t * decs + i, :, 0:doc_rows] = stat[:, i * doc_rows:(i + 1) * doc_rows]

    got_dec[dec] = stats[dec]
    for d in range(1, dec_n):
        to = flip(dec, d)
        pltpu.make_async_remote_copy(
            src_ref=stats.at[to], dst_ref=got_dec.at[dec], send_sem=dec_send,
            recv_sem=dec_recv, device_id=(to, tp), device_id_type=MESH).start()
    come = pltpu.make_async_copy(got_dec.at[0:dec_n - 1], got_dec.at[0:dec_n - 1], dec_recv)
    come.wait()

    def merged(got):
        peak = jnp.max(got[:, 0:1, :], axis=0)
        summed = jnp.sum(got[:, 1:2, :] * jnp.exp(got[:, 0:1, :] - peak[None]), axis=0)
        return peak, summed, jnp.sum(got[:, 2:3, :], axis=0)

    for i, value in enumerate(merged(got_dec[...])):
        stat_doc[i:i + 1, :] = value
    got_tp[tp] = stat_doc[...]
    for d in range(1, tp_n):
        pltpu.make_async_remote_copy(
            src_ref=stat_doc, dst_ref=got_tp.at[tp], send_sem=tp_send,
            recv_sem=tp_recv, device_id=(dec, flip(tp, d)), device_id_type=MESH).start()
    pltpu.make_async_copy(got_tp.at[0:tp_n - 1], got_tp.at[0:tp_n - 1], tp_recv).wait()
    peak, summed, target = merged(got_tp[...])

    logp = target - (peak + jnp.log(summed))
    score = logp
    for l in range(1, length):
        score = score + pltpu.roll(logp, 128 - l, 1)
    score = score / length
    lane = lax.broadcasted_iota(jnp.int32, (1, 128), 1)
    first = jnp.logical_and(lane % length == 0, lane < doc_rows)
    alive = jnp.logical_and(first, lane // length < counts[0])
    best = jnp.max(jnp.where(alive, score, -jnp.inf), axis=1, keepdims=True)
    norm = best + jnp.log(jnp.sum(
        jnp.exp(jnp.where(alive, score - best, -jnp.inf)), axis=1, keepdims=True))
    hyp = jnp.where(alive, score, 0.0)
    post = jnp.where(alive, score - norm, 0.0)
    out_lane = lax.broadcasted_iota(jnp.int32, (1, slots), 1)
    hyp_out = jnp.zeros((1, slots), jnp.float32)
    post_out = jnp.zeros((1, slots), jnp.float32)
    for s in range(slots):
        here = lane == (tp * slots + s) * length
        hyp_out = jnp.where(out_lane == s, jnp.sum(jnp.where(here, hyp, 0.0), axis=1, keepdims=True), hyp_out)
        post_out = jnp.where(out_lane == s, jnp.sum(jnp.where(here, post, 0.0), axis=1, keepdims=True), post_out)
    hyp_ref[...] = hyp_out
    post_ref[...] = post_out

    wait(rows.at[0:z_n - 1, 0, 0], z_send)
    for sem in (u_send, v_send):
        wait(rows.at[:, 0, 0:x_n - 1], sem)
    for sem, piece in ((uv_send, low), (vu_send, high)):
        wait(rows.at[:, 0, 0:(x_n - 1) ** 2, :, piece], sem)
    wait(rows.at[:, 0], mate_send)
    pltpu.make_async_copy(got_dec.at[0:dec_n - 1], got_dec.at[0:dec_n - 1], dec_send).wait()
    pltpu.make_async_copy(got_tp.at[0:tp_n - 1], got_tp.at[0:tp_n - 1], tp_send).wait()


def body(dec_n, tp_n, hidden, norm_gain, lm_head, token_ids, doc_counts):
    slots, length, width = hidden.shape[1:]
    own_rows = slots * length
    vocab = lm_head.shape[0]
    doc_rows = tp_n * own_rows
    decs = max(1, min(256, dec_n * doc_rows) // doc_rows)
    all_slots = token_ids.shape[1]
    vmem = pl.BlockSpec(memory_space=pltpu.VMEM)
    out = jax.ShapeDtypeStruct((1, slots), jnp.float32)
    dma = pltpu.SemaphoreType.DMA
    side = 2 ** (tp_n.bit_length() // 2)
    return pl.pallas_call(
        functools.partial(kernel, dec_n, tp_n),
        out_shape=(out, out),
        in_specs=[pl.BlockSpec(memory_space=pl.ANY)] * 4 + [pl.BlockSpec(memory_space=pltpu.SMEM)],
        out_specs=(vmem, vmem),
        scratch_shapes=[
            pltpu.VMEM(hidden.shape, jnp.float32),
            pltpu.VMEM((1, width), jnp.float32),
            pltpu.VMEM((1, length, all_slots), jnp.int32),
            pltpu.VMEM((vocab, width), jnp.bfloat16),
            pltpu.VMEM((dec_n // CORES, CORES, tp_n, HALVES * own_rows, width // HALVES + ID_LANES), jnp.bfloat16),
            pltpu.VMEM((own_rows, width), jnp.float32),
            pltpu.VMEM((vocab, decs * doc_rows), jnp.float32),
            pltpu.VMEM((dec_n, 8, 128), jnp.float32),
            pltpu.VMEM((dec_n, 8, 128), jnp.float32),
            pltpu.VMEM((8, 128), jnp.float32),
            pltpu.VMEM((tp_n, 8, 128), jnp.float32),
            dma, dma, dma, dma, dma, dma((2,)), dma, dma((2, side)), dma, dma((2, side)),
            dma, dma((2, side, side)), dma, dma((2, side, side)), dma, dma((2,)),
            dma, dma, dma, dma,
        ],
        compiler_params=pltpu.CompilerParams(
            collective_id=0, has_side_effects=True, vmem_limit_bytes=60 * 1024 * 1024),
        name="rescore",
    )(hidden, norm_gain.reshape(1, width), lm_head, jnp.swapaxes(token_ids, 1, 2), doc_counts)


def solution(mesh):
    placed = (
        P("dec", "tp", None, None),
        P(),
        P(("dec", "tp"), None),
        P("dec", None, None),
        P("dec"),
    )
    return jax.shard_map(
        functools.partial(body, mesh.shape["dec"], mesh.shape["tp"]),
        mesh=mesh,
        in_specs=placed,
        out_specs=(P("dec", "tp"), P("dec", "tp")),
        check_vma=False,
    )
```

```python
import functools

import jax
import jax.numpy as jnp
from jax import lax
from jax.experimental import pallas as pl
from jax.experimental.pallas import tpu as pltpu
from jax.sharding import PartitionSpec as P

MESH = pl.DeviceIdType.MESH
CORES = 2
HALVES = 2
ID_LANES = 128
EPS = 1e-05


def flip(index, mask):
    bit = 1
    while bit <= mask:
        if mask & bit:
            index = index + bit - 2 * bit * ((index // bit) % 2)
        bit *= 2
    return index


def kernel(dec_n, tp_n, hidden_hbm, gain_hbm, lm_head, ids_hbm, counts, hyp_ref, post_ref,
           hidden, gain, ids, weights, rows, fresh, logits, stats, got_dec, stat_doc, got_tp,
           h_sem, g_sem, i_sem, w_sem, z_send, z_recv, u_send, u_recv, v_send, v_recv,
           uv_send, uv_recv, vu_send, vu_recv, mate_send, mate_recv, dec_send, dec_recv, tp_send, tp_recv):
    slots, length, width = hidden.shape[1:]
    own_rows = slots * length
    doc_rows = tp_n * own_rows
    vocab = lm_head.shape[0]
    z_n = dec_n // CORES
    x_n = 2 ** ((tp_n.bit_length()) // 2)
    assert x_n * x_n == tp_n
    half = width // HALVES
    piece_width = half // HALVES
    z_half = z_n // 2
    dec, tp = lax.axis_index("dec"), lax.axis_index("tp")
    z, core = dec // CORES, dec % CORES
    u_step = 1 + core * (x_n - 1)
    v_step = x_n - core * (x_n - 1)
    u, v = (tp // u_step) % x_n, (tp // v_step) % x_n

    loads = [pltpu.make_async_copy(*pair) for pair in (
        (hidden_hbm, hidden, h_sem), (gain_hbm, gain, g_sem), (ids_hbm, ids, i_sem), (lm_head, weights, w_sem))]
    for load in loads:
        load.start()
    barrier = pltpu.get_barrier_semaphore()
    for d in range(1, dec_n):
        pl.semaphore_signal(barrier, inc=1, device_id=(flip(dec, d), tp), device_id_type=MESH)
    for d in range(1, tp_n):
        pl.semaphore_signal(barrier, inc=1, device_id=(dec, flip(tp, d)), device_id_type=MESH)
    for load in loads[:3]:
        load.wait()

    for s in range(slots):
        part = hidden[0, s]
        meansq = jnp.mean(part * part, axis=1, keepdims=True)
        fresh[s * length:(s + 1) * length, :] = part * lax.rsqrt(meansq + EPS) * gain[...]
    rows[z, core, tp, :, 0:half] = jnp.concatenate(
        [fresh[:, 0:half], fresh[:, half:width]], axis=0).astype(jnp.bfloat16)

    lane = lax.broadcasted_iota(jnp.int32, (length, ID_LANES), 1)
    slot = lax.broadcasted_iota(jnp.int32, ids.shape[1:], 1)
    digits = []
    for s in range(slots):
        here = jnp.where(slot == tp * slots + s, ids[0], 0).astype(jnp.float32)
        token = jnp.sum(here, axis=1, keepdims=True).astype(jnp.int32)
        shift = jnp.where(lane == 0, 12, jnp.where(lane == 1, 6, 0))
        digit = jnp.bitwise_and(jnp.right_shift(jnp.broadcast_to(token, lane.shape), shift), 63)
        digits.append(jnp.where(lane < 3, digit, 0).astype(jnp.float32))
    digits.append(jnp.zeros((own_rows, ID_LANES), jnp.float32))
    rows[z, core, tp, :, half:half + ID_LANES] = jnp.concatenate(digits, axis=0).astype(jnp.bfloat16)
    stats[...] = jnp.zeros_like(stats)
    stat_doc[...] = jnp.zeros_like(stat_doc)

    pl.semaphore_wait(barrier, dec_n + tp_n - 2)

    def place(vv, uu):
        return vv * v_step + uu * u_step

    def send(piece, send_sem, recv_sem, to_dec, to_tp):
        pltpu.make_async_remote_copy(
            src_ref=piece, dst_ref=piece, send_sem=send_sem, recv_sem=recv_sem,
            device_id=(to_dec, to_tp), device_id_type=MESH).start()

    def wait(piece, sem):
        pltpu.make_async_copy(piece, piece, sem).wait()

    first_z = (z // z_half) * z_half
    groups = [pl.ds(first_z, z_half), pl.ds(z_half - first_z, z_half)]
    low, high = pl.ds(0, piece_width), pl.ds(piece_width, piece_width + ID_LANES)
    near = range(1, x_n)

    for d in range(1, z_n):
        send(rows.at[z, core, tp], z_send, z_recv.at[d // z_half], flip(z, d) * CORES + core, tp)
    def send_near(piece, g):
        for e in near:
            send(piece, u_send, u_recv.at[g, e], dec, place(v, flip(u, e)))
            send(piece, v_send, v_recv.at[g, e], dec, place(flip(v, e), u))

    def send_mate(piece, g):
        send(piece, mate_send, mate_recv.at[g], flip(dec, 1), tp)

    send_near(rows.at[z, core, tp], 0)
    for g, group in enumerate(groups):
        wait(rows.at[pl.ds(0, z_half - 1 + g), core, tp], z_recv.at[g])
        if g == 0:
            for d in range(1, z_half):
                send_near(rows.at[flip(z, d), core, tp], g)
        else:
            send_near(rows.at[group, core, tp], g)
        send_mate(rows.at[group, core, tp], g)
    for g, group in enumerate(groups):
        for e in near:
            at = place(v, flip(u, e))
            wait(rows.at[group, core, at], u_recv.at[g, e])
            for f in near:
                send(rows.at[group, core, at, :, low], uv_send, uv_recv.at[g, e, f], dec, place(flip(v, f), u))
            send_mate(rows.at[group, core, at], g)
            at = place(flip(v, e), u)
            wait(rows.at[group, core, at], v_recv.at[g, e])
            for f in near:
                send(rows.at[group, core, at, :, high], vu_send, vu_recv.at[g, f, e], dec, place(v, flip(u, f)))
            send_mate(rows.at[group, core, at], g)
    for g, group in enumerate(groups):
        for e in near:
            for f in near:
                at = place(flip(v, f), flip(u, e))
                wait(rows.at[group, core, at, :, low], uv_recv.at[g, e, f])
                wait(rows.at[group, core, at, :, high], vu_recv.at[g, e, f])
                send_mate(rows.at[group, core, at], g)
    loads[3].wait()

    decs = max(1, min(256, dec_n * doc_rows) // doc_rows)
    tile = decs * doc_rows
    step = 1024
    flat = rows.reshape(dec_n, tp_n, 2 * own_rows, half + ID_LANES)
    vocab_start = (dec * tp_n + tp) * vocab
    column = lax.broadcasted_iota(jnp.int32, (8, ID_LANES), 1)
    scale = jnp.where(column == 0, 4096.0, jnp.where(column == 1, 64.0, jnp.where(column == 2, 1.0, 0.0)))

    def times_rows(left, right):
        return lax.dot_general(left, right.reshape(tile, right.shape[-1]).astype(jnp.bfloat16),
                               (((1,), (1,)), ((), ())), preferred_element_type=jnp.float32)

    for g, group in enumerate(groups):
        wait(rows.at[group, 1 - core], mate_recv.at[g])

    @pl.loop(0, dec_n // decs)
    def _(t):
        logits[...] = jnp.zeros((vocab, tile), jnp.float32)
        some = pl.ds(t * decs, decs)

        @pl.loop(0, half // step)
        def _(k):
            at = pl.ds(pl.multiple_of(k * step, step), step)
            beyond = pl.ds(pl.multiple_of(k * step + half, step), step)
            both = flat[some, :, :, at].astype(jnp.float32)
            logits[...] += (times_rows(weights[:, at], both[:, :, 0:own_rows])
                            + times_rows(weights[:, beyond], both[:, :, own_rows:2 * own_rows]))

        tail = flat[some, :, :, pl.ds(half, ID_LANES)].astype(jnp.float32)
        row_ids = times_rows(scale.astype(jnp.bfloat16), tail[:, :, 0:own_rows])[0:1, :]
        value = logits[...]
        peak = jnp.max(value, axis=0, keepdims=True)
        summed = jnp.sum(jnp.exp(value - peak), axis=0, keepdims=True)
        entry = (lax.broadcasted_iota(jnp.int32, (vocab, tile), 0) + vocab_start).astype(jnp.float32)
        target = jnp.sum(jnp.where(entry == row_ids, value, 0.0), axis=0, keepdims=True)
        which = lax.broadcasted_iota(jnp.int32, (8, tile), 0)
        stat = jnp.where(which == 0, peak, jnp.where(which == 1, summed, target))
        for i in range(decs):
            stats[t * decs + i, :, 0:doc_rows] = stat[:, i * doc_rows:(i + 1) * doc_rows]

    got_dec[dec] = stats[dec]
    for d in range(1, dec_n):
        to = flip(dec, d)
        pltpu.make_async_remote_copy(
            src_ref=stats.at[to], dst_ref=got_dec.at[dec], send_sem=dec_send,
            recv_sem=dec_recv, device_id=(to, tp), device_id_type=MESH).start()
    come = pltpu.make_async_copy(got_dec.at[0:dec_n - 1], got_dec.at[0:dec_n - 1], dec_recv)
    come.wait()

    def merged(got):
        peak = jnp.max(got[:, 0:1, :], axis=0)
        summed = jnp.sum(got[:, 1:2, :] * jnp.exp(got[:, 0:1, :] - peak[None]), axis=0)
        return peak, summed, jnp.sum(got[:, 2:3, :], axis=0)

    for i, value in enumerate(merged(got_dec[...])):
        stat_doc[i:i + 1, :] = value
    got_tp[tp] = stat_doc[...]
    for d in range(1, tp_n):
        pltpu.make_async_remote_copy(
            src_ref=stat_doc, dst_ref=got_tp.at[tp], send_sem=tp_send,
            recv_sem=tp_recv, device_id=(dec, flip(tp, d)), device_id_type=MESH).start()
    pltpu.make_async_copy(got_tp.at[0:tp_n - 1], got_tp.at[0:tp_n - 1], tp_recv).wait()
    peak, summed, target = merged(got_tp[...])

    logp = target - (peak + jnp.log(summed))
    score = logp
    for l in range(1, length):
        score = score + pltpu.roll(logp, 128 - l, 1)
    score = score / length
    lane = lax.broadcasted_iota(jnp.int32, (1, 128), 1)
    first = jnp.logical_and(lane % length == 0, lane < doc_rows)
    alive = jnp.logical_and(first, lane // length < counts[0])
    best = jnp.max(jnp.where(alive, score, -jnp.inf), axis=1, keepdims=True)
    norm = best + jnp.log(jnp.sum(
        jnp.exp(jnp.where(alive, score - best, -jnp.inf)), axis=1, keepdims=True))
    hyp = jnp.where(alive, score, 0.0)
    post = jnp.where(alive, score - norm, 0.0)
    out_lane = lax.broadcasted_iota(jnp.int32, (1, slots), 1)
    hyp_out = jnp.zeros((1, slots), jnp.float32)
    post_out = jnp.zeros((1, slots), jnp.float32)
    for s in range(slots):
        here = lane == (tp * slots + s) * length
        hyp_out = jnp.where(out_lane == s, jnp.sum(jnp.where(here, hyp, 0.0), axis=1, keepdims=True), hyp_out)
        post_out = jnp.where(out_lane == s, jnp.sum(jnp.where(here, post, 0.0), axis=1, keepdims=True), post_out)
    hyp_ref[...] = hyp_out
    post_ref[...] = post_out

    wait(rows.at[0:z_n - 1, 0, 0], z_send)
    for sem in (u_send, v_send):
        wait(rows.at[:, 0, 0:x_n - 1], sem)
    for sem, piece in ((uv_send, low), (vu_send, high)):
        wait(rows.at[:, 0, 0:(x_n - 1) ** 2, :, piece], sem)
    wait(rows.at[:, 0], mate_send)
    pltpu.make_async_copy(got_dec.at[0:dec_n - 1], got_dec.at[0:dec_n - 1], dec_send).wait()
    pltpu.make_async_copy(got_tp.at[0:tp_n - 1], got_tp.at[0:tp_n - 1], tp_send).wait()


def body(dec_n, tp_n, hidden, norm_gain, lm_head, token_ids, doc_counts):
    slots, length, width = hidden.shape[1:]
    own_rows = slots * length
    vocab = lm_head.shape[0]
    doc_rows = tp_n * own_rows
    decs = max(1, min(256, dec_n * doc_rows) // doc_rows)
    all_slots = token_ids.shape[1]
    vmem = pl.BlockSpec(memory_space=pltpu.VMEM)
    out = jax.ShapeDtypeStruct((1, slots), jnp.float32)
    dma = pltpu.SemaphoreType.DMA
    side = 2 ** (tp_n.bit_length() // 2)
    return pl.pallas_call(
        functools.partial(kernel, dec_n, tp_n),
        out_shape=(out, out),
        in_specs=[pl.BlockSpec(memory_space=pl.ANY)] * 4 + [pl.BlockSpec(memory_space=pltpu.SMEM)],
        out_specs=(vmem, vmem),
        scratch_shapes=[
            pltpu.VMEM(hidden.shape, jnp.float32),
            pltpu.VMEM((1, width), jnp.float32),
            pltpu.VMEM((1, length, all_slots), jnp.int32),
            pltpu.VMEM((vocab, width), jnp.bfloat16),
            pltpu.VMEM((dec_n // CORES, CORES, tp_n, HALVES * own_rows, width // HALVES + ID_LANES), jnp.bfloat16),
            pltpu.VMEM((own_rows, width), jnp.float32),
            pltpu.VMEM((vocab, decs * doc_rows), jnp.float32),
            pltpu.VMEM((dec_n, 8, 128), jnp.float32),
            pltpu.VMEM((dec_n, 8, 128), jnp.float32),
            pltpu.VMEM((8, 128), jnp.float32),
            pltpu.VMEM((tp_n, 8, 128), jnp.float32),
            dma, dma, dma, dma, dma, dma((2,)), dma, dma((2, side)), dma, dma((2, side)),
            dma, dma((2, side, side)), dma, dma((2, side, side)), dma, dma((2,)),
            dma, dma, dma, dma,
        ],
        compiler_params=pltpu.CompilerParams(
            collective_id=0, has_side_effects=True, vmem_limit_bytes=60 * 1024 * 1024),
        name="rescore",
    )(hidden, norm_gain.reshape(1, width), lm_head, jnp.swapaxes(token_ids, 1, 2), doc_counts)


def solution(mesh):
    placed = (
        P("dec", "tp", None, None),
        P(),
        P(("dec", "tp"), None),
        P("dec", None, None),
        P("dec"),
    )
    return jax.shard_map(
        functools.partial(body, mesh.shape["dec"], mesh.shape["tp"]),
        mesh=mesh,
        in_specs=placed,
        out_specs=(P("dec", "tp"), P("dec", "tp")),
        check_vma=False,
    )
```

```python
import functools

import jax
import jax.numpy as jnp
from jax import lax
from jax.experimental import pallas as pl
from jax.experimental.pallas import tpu as pltpu
from jax.sharding import PartitionSpec as P

MESH = pl.DeviceIdType.MESH
CORES = 2
HALVES = 2
ID_LANES = 128
EPS = 1e-05


def flip(index, mask):
    bit = 1
    while bit <= mask:
        if mask & bit:
            index = index + bit - 2 * bit * ((index // bit) % 2)
        bit *= 2
    return index


def kernel(dec_n, tp_n, hidden_hbm, gain_hbm, lm_head, ids_hbm, counts, out_ref,
           hidden, gain, ids, weights, rows, fresh, logits, stats, got_dec, stat_doc, got_tp,
           h_sem, g_sem, i_sem, w_sem, z_send, z_recv, u_send, u_recv, v_send, v_recv,
           uv_send, uv_recv, vu_send, vu_recv, mate_send, mate_recv, dec_send, dec_recv, tp_send, tp_recv):
    slots, length, width = hidden.shape[1:]
    own_rows = slots * length
    doc_rows = tp_n * own_rows
    vocab = lm_head.shape[0]
    z_n = dec_n // CORES
    x_n = 2 ** ((tp_n.bit_length()) // 2)
    assert x_n * x_n == tp_n
    half = width // HALVES
    piece_width = half // HALVES
    z_half = z_n // 2
    dec, tp = lax.axis_index("dec"), lax.axis_index("tp")
    z, core = dec // CORES, dec % CORES
    u_step = 1 + core * (x_n - 1)
    v_step = x_n - core * (x_n - 1)
    u, v = (tp // u_step) % x_n, (tp // v_step) % x_n

    loads = [pltpu.make_async_copy(*pair) for pair in (
        (hidden_hbm, hidden, h_sem), (gain_hbm, gain, g_sem), (ids_hbm, ids, i_sem), (lm_head, weights, w_sem))]
    for load in loads:
        load.start()
    barrier = pltpu.get_barrier_semaphore()
    for d in range(1, dec_n):
        pl.semaphore_signal(barrier, inc=1, device_id=(flip(dec, d), tp), device_id_type=MESH)
    for d in range(1, tp_n):
        pl.semaphore_signal(barrier, inc=1, device_id=(dec, flip(tp, d)), device_id_type=MESH)
    for load in loads[:3]:
        load.wait()

    for s in range(slots):
        part = hidden[0, s]
        meansq = jnp.mean(part * part, axis=1, keepdims=True)
        fresh[s * length:(s + 1) * length, :] = part * lax.rsqrt(meansq + EPS) * gain[...]
    rows[z, core, tp, :, 0:half] = jnp.concatenate(
        [fresh[:, 0:half], fresh[:, half:width]], axis=0).astype(jnp.bfloat16)

    lane = lax.broadcasted_iota(jnp.int32, (length, ID_LANES), 1)
    slot = lax.broadcasted_iota(jnp.int32, ids.shape[1:], 1)
    digits = []
    for s in range(slots):
        here = jnp.where(slot == tp * slots + s, ids[0], 0).astype(jnp.float32)
        token = jnp.sum(here, axis=1, keepdims=True).astype(jnp.int32)
        shift = jnp.where(lane == 0, 12, jnp.where(lane == 1, 6, 0))
        digit = jnp.bitwise_and(jnp.right_shift(jnp.broadcast_to(token, lane.shape), shift), 63)
        digits.append(jnp.where(lane < 3, digit, 0).astype(jnp.float32))
    digits.append(jnp.zeros((own_rows, ID_LANES), jnp.float32))
    rows[z, core, tp, :, half:half + ID_LANES] = jnp.concatenate(digits, axis=0).astype(jnp.bfloat16)
    stats[...] = jnp.zeros_like(stats)
    stat_doc[...] = jnp.zeros_like(stat_doc)

    pl.semaphore_wait(barrier, dec_n + tp_n - 2)

    def place(vv, uu):
        return vv * v_step + uu * u_step

    def send(piece, send_sem, recv_sem, to_dec, to_tp):
        pltpu.make_async_remote_copy(
            src_ref=piece, dst_ref=piece, send_sem=send_sem, recv_sem=recv_sem,
            device_id=(to_dec, to_tp), device_id_type=MESH).start()

    def wait(piece, sem):
        pltpu.make_async_copy(piece, piece, sem).wait()

    first_z = (z // z_half) * z_half
    groups = [pl.ds(first_z, z_half), pl.ds(z_half - first_z, z_half)]
    low, high = pl.ds(0, piece_width), pl.ds(piece_width, piece_width + ID_LANES)
    near = range(1, x_n)

    for d in range(1, z_n):
        send(rows.at[z, core, tp], z_send, z_recv.at[d // z_half], flip(z, d) * CORES + core, tp)
    def send_near(piece, g):
        for e in near:
            send(piece, u_send, u_recv.at[g, e], dec, place(v, flip(u, e)))
            send(piece, v_send, v_recv.at[g, e], dec, place(flip(v, e), u))

    def send_mate(piece, g):
        send(piece, mate_send, mate_recv.at[g], flip(dec, 1), tp)

    send_near(rows.at[z, core, tp], 0)
    for g, group in enumerate(groups):
        wait(rows.at[pl.ds(0, z_half - 1 + g), core, tp], z_recv.at[g])
        if g == 0:
            for d in range(1, z_half):
                send_near(rows.at[flip(z, d), core, tp], g)
        else:
            send_near(rows.at[group, core, tp], g)
        send_mate(rows.at[group, core, tp], g)
    for g, group in enumerate(groups):
        for e in near:
            at = place(v, flip(u, e))
            wait(rows.at[group, core, at], u_recv.at[g, e])
            for f in near:
                send(rows.at[group, core, at, :, low], uv_send, uv_recv.at[g, e, f], dec, place(flip(v, f), u))
            send_mate(rows.at[group, core, at], g)
            at = place(flip(v, e), u)
            wait(rows.at[group, core, at], v_recv.at[g, e])
            for f in near:
                send(rows.at[group, core, at, :, high], vu_send, vu_recv.at[g, f, e], dec, place(v, flip(u, f)))
            send_mate(rows.at[group, core, at], g)
    for g, group in enumerate(groups):
        for e in near:
            for f in near:
                at = place(flip(v, f), flip(u, e))
                wait(rows.at[group, core, at, :, low], uv_recv.at[g, e, f])
                wait(rows.at[group, core, at, :, high], vu_recv.at[g, e, f])
                send_mate(rows.at[group, core, at], g)
    loads[3].wait()

    decs = max(1, min(256, dec_n * doc_rows) // doc_rows)
    tile = decs * doc_rows
    step = 1024
    flat = rows.reshape(dec_n, tp_n, 2 * own_rows, half + ID_LANES)
    vocab_start = (dec * tp_n + tp) * vocab
    column = lax.broadcasted_iota(jnp.int32, (8, ID_LANES), 1)
    scale = jnp.where(column == 0, 4096.0, jnp.where(column == 1, 64.0, jnp.where(column == 2, 1.0, 0.0)))

    def times_rows(left, right):
        return lax.dot_general(left, right.reshape(tile, right.shape[-1]).astype(jnp.bfloat16),
                               (((1,), (1,)), ((), ())), preferred_element_type=jnp.float32)

    for g, group in enumerate(groups):
        wait(rows.at[group, 1 - core], mate_recv.at[g])

    @pl.loop(0, dec_n // decs)
    def _(t):
        logits[...] = jnp.zeros((vocab, tile), jnp.float32)
        some = pl.ds(t * decs, decs)

        @pl.loop(0, half // step)
        def _(k):
            at = pl.ds(pl.multiple_of(k * step, step), step)
            beyond = pl.ds(pl.multiple_of(k * step + half, step), step)
            both = flat[some, :, :, at].astype(jnp.float32)
            logits[...] += (times_rows(weights[:, at], both[:, :, 0:own_rows])
                            + times_rows(weights[:, beyond], both[:, :, own_rows:2 * own_rows]))

        tail = flat[some, :, :, pl.ds(half, ID_LANES)].astype(jnp.float32)
        row_ids = times_rows(scale.astype(jnp.bfloat16), tail[:, :, 0:own_rows])[0:1, :]
        value = logits[...]
        peak = jnp.max(value, axis=0, keepdims=True)
        summed = jnp.sum(jnp.exp(value - peak), axis=0, keepdims=True)
        entry = (lax.broadcasted_iota(jnp.int32, (vocab, tile), 0) + vocab_start).astype(jnp.float32)
        target = jnp.sum(jnp.where(entry == row_ids, value, 0.0), axis=0, keepdims=True)
        which = lax.broadcasted_iota(jnp.int32, (8, tile), 0)
        stat = jnp.where(which == 0, peak, jnp.where(which == 1, summed, target))
        for i in range(decs):
            stats[t * decs + i, :, 0:doc_rows] = stat[:, i * doc_rows:(i + 1) * doc_rows]

    got_dec[dec] = stats[dec]
    for d in range(1, dec_n):
        to = flip(dec, d)
        pltpu.make_async_remote_copy(
            src_ref=stats.at[to], dst_ref=got_dec.at[dec], send_sem=dec_send,
            recv_sem=dec_recv, device_id=(to, tp), device_id_type=MESH).start()
    come = pltpu.make_async_copy(got_dec.at[0:dec_n - 1], got_dec.at[0:dec_n - 1], dec_recv)
    come.wait()

    def merged(got):
        peak = jnp.max(got[:, 0:1, :], axis=0)
        summed = jnp.sum(got[:, 1:2, :] * jnp.exp(got[:, 0:1, :] - peak[None]), axis=0)
        return peak, summed, jnp.sum(got[:, 2:3, :], axis=0)

    for i, value in enumerate(merged(got_dec[...])):
        stat_doc[i:i + 1, :] = value
    got_tp[tp] = stat_doc[...]
    for d in range(1, tp_n):
        pltpu.make_async_remote_copy(
            src_ref=stat_doc, dst_ref=got_tp.at[tp], send_sem=tp_send,
            recv_sem=tp_recv, device_id=(dec, flip(tp, d)), device_id_type=MESH).start()
    pltpu.make_async_copy(got_tp.at[0:tp_n - 1], got_tp.at[0:tp_n - 1], tp_recv).wait()
    peak, summed, target = merged(got_tp[...])

    logp = target - (peak + jnp.log(summed))
    score = logp
    for l in range(1, length):
        score = score + pltpu.roll(logp, 128 - l, 1)
    score = score / length
    lane = lax.broadcasted_iota(jnp.int32, (1, 128), 1)
    first = jnp.logical_and(lane % length == 0, lane < doc_rows)
    alive = jnp.logical_and(first, lane // length < counts[0])
    best = jnp.max(jnp.where(alive, score, -jnp.inf), axis=1, keepdims=True)
    norm = best + jnp.log(jnp.sum(
        jnp.exp(jnp.where(alive, score - best, -jnp.inf)), axis=1, keepdims=True))
    hyp = jnp.where(alive, score, 0.0)
    post = jnp.where(alive, score - norm, 0.0)
    out_lane = lax.broadcasted_iota(jnp.int32, (1, slots), 1)
    hyp_out = jnp.zeros((1, slots), jnp.float32)
    post_out = jnp.zeros((1, slots), jnp.float32)
    for s in range(slots):
        here = lane == (tp * slots + s) * length
        hyp_out = jnp.where(out_lane == s, jnp.sum(jnp.where(here, hyp, 0.0), axis=1, keepdims=True), hyp_out)
        post_out = jnp.where(out_lane == s, jnp.sum(jnp.where(here, post, 0.0), axis=1, keepdims=True), post_out)
    out_ref[0:1, :] = hyp_out
    out_ref[1:2, :] = post_out

    wait(rows.at[0:z_n - 1, 0, 0], z_send)
    for sem in (u_send, v_send):
        wait(rows.at[:, 0, 0:x_n - 1], sem)
    for sem, piece in ((uv_send, low), (vu_send, high)):
        wait(rows.at[:, 0, 0:(x_n - 1) ** 2, :, piece], sem)
    wait(rows.at[:, 0], mate_send)
    pltpu.make_async_copy(got_dec.at[0:dec_n - 1], got_dec.at[0:dec_n - 1], dec_send).wait()
    pltpu.make_async_copy(got_tp.at[0:tp_n - 1], got_tp.at[0:tp_n - 1], tp_send).wait()


def body(dec_n, tp_n, hidden, norm_gain, lm_head, token_ids, doc_counts):
    slots, length, width = hidden.shape[1:]
    own_rows = slots * length
    vocab = lm_head.shape[0]
    doc_rows = tp_n * own_rows
    decs = max(1, min(256, dec_n * doc_rows) // doc_rows)
    all_slots = token_ids.shape[1]
    vmem = pl.BlockSpec(memory_space=pltpu.VMEM)
    out = jax.ShapeDtypeStruct((2, slots), jnp.float32)
    dma = pltpu.SemaphoreType.DMA
    side = 2 ** (tp_n.bit_length() // 2)
    scores = pl.pallas_call(
        functools.partial(kernel, dec_n, tp_n),
        out_shape=out,
        in_specs=[pl.BlockSpec(memory_space=pl.ANY)] * 4 + [pl.BlockSpec(memory_space=pltpu.SMEM)],
        out_specs=vmem,
        scratch_shapes=[
            pltpu.VMEM(hidden.shape, jnp.float32),
            pltpu.VMEM((1, width), jnp.float32),
            pltpu.VMEM((1, length, all_slots), jnp.int32),
            pltpu.VMEM((vocab, width), jnp.bfloat16),
            pltpu.VMEM((dec_n // CORES, CORES, tp_n, HALVES * own_rows, width // HALVES + ID_LANES), jnp.bfloat16),
            pltpu.VMEM((own_rows, width), jnp.float32),
            pltpu.VMEM((vocab, decs * doc_rows), jnp.float32),
            pltpu.VMEM((dec_n, 8, 128), jnp.float32),
            pltpu.VMEM((dec_n, 8, 128), jnp.float32),
            pltpu.VMEM((8, 128), jnp.float32),
            pltpu.VMEM((tp_n, 8, 128), jnp.float32),
            dma, dma, dma, dma, dma, dma((2,)), dma, dma((2, side)), dma, dma((2, side)),
            dma, dma((2, side, side)), dma, dma((2, side, side)), dma, dma((2,)),
            dma, dma, dma, dma,
        ],
        compiler_params=pltpu.CompilerParams(
            collective_id=0, has_side_effects=True, vmem_limit_bytes=60 * 1024 * 1024),
        name="rescore",
    )(hidden, norm_gain.reshape(1, width), lm_head, jnp.swapaxes(token_ids, 1, 2), doc_counts)
    return scores[0:1], scores[1:2]


def solution(mesh):
    placed = (
        P("dec", "tp", None, None),
        P(),
        P(("dec", "tp"), None),
        P("dec", None, None),
        P("dec"),
    )
    return jax.shard_map(
        functools.partial(body, mesh.shape["dec"], mesh.shape["tp"]),
        mesh=mesh,
        in_specs=placed,
        out_specs=(P("dec", "tp"), P("dec", "tp")),
        check_vma=False,
    )
```
